256 devices in a mesh: gx: 16 (over x_lo, z), gy: 2 (over x_hi), gz: 8 (over y, core).
Axes of the slice: x: 4 (x_hi: 2, x_lo: 2; x = x_hi * 2 + x_lo), y: 4, z: 8, core: 2. Of those that a mesh axis runs over, the one named last changes fastest.
Arguments:
- normed: bfloat16 [1024, 6144], P(('gy', 'gz'), 'gx'), may hold values from -6 to 6
- w_in: bfloat16 [6144, 24576], P('gx', ('gz', 'gy')), may hold values from -0.078125 to 0.078125
- w_out: bfloat16 [24576, 6144], P(('gz', 'gy'), 'gx'), may hold values from -0.0390625 to 0.0390625
- cotangent: bfloat16 [1024, 6144], P(('gy', 'gz'), 'gx'), may hold values from -6 to 6
Outputs:
- block_out: bfloat16 [1024, 6144], P(('gy', 'gz'), 'gx')
- grad_input: bfloat16 [1024, 6144], P(('gy', 'gz'), 'gx')
- grad_w_in: bfloat16 [6144, 24576], P('gx', ('gz', 'gy'))
- grad_w_out: bfloat16 [24576, 6144], P(('gz', 'gy'), 'gx')
The draws below stay inside these ranges and needn't reach their ends.
All inputs are finite; a program needn't handle non-finite values.
Results may differ from the reference program's by a relative error of at most 0.0049.
Values may be sent and summed in bfloat16 or wider, within the bound.
A program may use at most 128 MiB of HBM per device.

```python
import math
import jax
import jax.numpy as jnp

D = 6144
FF = 24576
TOKENS = 1024


def with_spikes(array, key, source, target, shards_of, factor):
    owner, partner = [(jnp.arange(array.shape[position]) // (array.shape[position] // shards_of)).reshape([-1 if axis == position else 1 for axis in range(array.ndim)]) for position in (source, target)]
    chosen = jax.random.permutation(key, shards_of)[partner]
    strong = (owner == chosen) | (owner == (partner + shards_of // 2) % shards_of)
    return jnp.where(strong, factor * array, array)


def steps_of(own_key, dims, cuts, low, largest):
    gain = 1.0
    for dim, blocks in cuts:
        heights = jax.random.uniform(jax.random.fold_in(jax.random.fold_in(own_key, 6), dim), (blocks,), jnp.float32, low / len(cuts), largest / len(cuts))
        gain = gain * jnp.repeat(jnp.exp(heights), dims[dim] // blocks).reshape((-1,) + (1,) * (len(dims) - 1 - dim))
    return gain


def noise(own_key, extent, deviation, bound, split=(), kind=jnp.bfloat16):
    result = deviation * jax.random.normal(own_key, extent, jnp.float32)
    if split:
        result = result * steps_of(own_key, extent, split, -0.22, 0.18)
    return jnp.clip(result, -bound, bound).astype(kind)


def noise_with(key, dims, scale, most, cuts, heavy, kind=jnp.bfloat16):
    result = scale * jax.random.normal(key, dims, jnp.float32)
    if cuts:
        result = result * steps_of(key, dims, cuts, -0.22, 0.18)
    return jnp.clip(with_spikes(result, jax.random.fold_in(key, 3), *heavy), -most, most).astype(kind)


def setup_inputs(seed: int = 0) -> dict:
    arg_keys = jax.random.split(jax.random.key(seed), 5)
    return {
        "normed": noise_with(arg_keys[0], (TOKENS, D), 1.0, 6.0, ((0, 16), (1, 16)), (1, 0, 16, 2.0)),
        "w_in": noise(arg_keys[1], (D, FF), D ** -0.5, 0.078125, ((0, 16), (1, 16))),
        "w_out": noise(arg_keys[2], (FF, D), FF ** -0.5, 0.0390625, ((0, 16), (1, 16))),
        "cotangent": noise_with(arg_keys[3], (TOKENS, D), 1.0, 6.0, ((0, 16), (1, 16)), (1, 0, 16, 2.0)),
    }


def gelu_value(v):
    return 0.5 * v * (1.0 + jax.scipy.special.erf(v / math.sqrt(2.0)))

def gelu_slope(v):
    return 0.5 * (1.0 + jax.scipy.special.erf(v / math.sqrt(2.0))) + v * jnp.exp(-0.5 * v * v) / math.sqrt(2.0 * math.pi)

def reference(normed, w_in, w_out, cotangent):
    preact = jnp.dot(normed, w_in, preferred_element_type=jnp.float32)
    hidden = gelu_value(preact).astype(jnp.bfloat16)
    block_out = jnp.dot(hidden, w_out, preferred_element_type=jnp.float32).astype(jnp.bfloat16)
    grad_hidden = jnp.dot(cotangent, w_out.T, preferred_element_type=jnp.float32)
    grad_pre = (grad_hidden * gelu_slope(preact)).astype(jnp.bfloat16)
    grad_input = jnp.dot(grad_pre, w_in.T, preferred_element_type=jnp.float32).astype(jnp.bfloat16)
    grad_w_in = jnp.dot(normed.T, grad_pre, preferred_element_type=jnp.float32).astype(jnp.bfloat16)
    grad_w_out = jnp.dot(hidden.T, cotangent, preferred_element_type=jnp.float32).astype(jnp.bfloat16)
    return (block_out, grad_input, grad_w_in, grad_w_out)
```

```python
import math

import jax
import jax.numpy as jnp
from jax import lax
from jax.experimental import pallas as pl
from jax.experimental.pallas import tpu as pltpu
from jax.sharding import PartitionSpec as P

BF = jnp.bfloat16
F32 = jnp.float32
MESH = pl.DeviceIdType.MESH

TOK = 1024
CHUNK = 128
DEPTH = 768
UNITS = 768
GROUP = 256
GROUPS = 3
STEPS = ((4, 3), (3, 4))


def gelu_value(v):
    return 0.5 * v * (1.0 + lax.erf(v / math.sqrt(2.0)))


def gelu_slope(v):
    return 0.5 * (1.0 + lax.erf(v / math.sqrt(2.0))) + v * jnp.exp(
        -0.5 * v * v
    ) / math.sqrt(2.0 * math.pi)


def dot(left, right, ldim=1, rdim=0):
    return lax.dot_general(
        left, right, (((ldim,), (rdim,)), ((), ())), preferred_element_type=F32
    )


def kernel(
    normed,
    w_in,
    w_out,
    cot,
    o_block,
    o_gin,
    o_gwin,
    o_gwout,
    acts,
    wi,
    wo,
    hid,
    slope,
    zsend,
    zrecv,
    outp,
    crecv,
    ysend0,
    yrecv0,
    ysend1,
    yrecv1,
    ysum,
    xsend,
    xrecv,
    gw,
    loc_sem,
    ag_send,
    ag_recv,
    w_send,
    w_recv,
    rs_send,
    rs_recv,
    za_send,
    za_recv,
    pl_send,
    pl_recv,
    gw_loc,
    gw_send,
    gw_recv,
):
    gx, gy, gz = lax.axis_index("gx"), lax.axis_index("gy"), lax.axis_index("gz")
    xl, z, xh, y, c = gx // 8, gx % 8, gy, gz // 2, gz % 2
    partner = ((1 - xl) * 8 + z, xh, gz)
    other = ((1 - xl) * 8 + z, 1 - xh, gz)
    zup = (xl * 8 + (z + 1) % 8, xh, gz)
    zdown = (xl * 8 + (z + 7) % 8, xh, gz)
    yup = (gx, xh, ((y + 1) % 4) * 2 + c)
    ydown = (gx, xh, ((y + 3) % 4) * 2 + c)
    sibling = (gx, xh, y * 2 + 1 - c)

    def send(src, dst, ssem, rsem, dev):
        return pltpu.make_async_remote_copy(
            src_ref=src,
            dst_ref=dst,
            send_sem=ssem,
            recv_sem=rsem,
            device_id=dev,
            device_id_type=MESH,
        )

    def arrived(ref, ssem, rsem):
        send(ref, ref, ssem, rsem, sibling).wait_recv()

    def left_here(ref, ssem, rsem):
        send(ref, ref, ssem, rsem, sibling).wait_send()

    def span(start, size, unit=128):
        return pl.ds(pl.multiple_of(start, unit), size)

    def chunk(k):
        return span(k * CHUNK, CHUNK)

    ins = (normed, cot)
    my_rows = span(((c * 4 + y) * 2 + xh) * 64, 64, 64)
    my_cols = span(xl * 384, 384)
    its_cols = span((1 - xl) * 384, 384)
    local = [
        pltpu.make_async_copy(ins[a], acts.at[a, my_rows, my_cols], loc_sem.at[a])
        for a in (0, 1)
    ]
    local.append(
        pltpu.make_async_copy(
            w_in.at[:, span(xl * 768, 768)], wi.at[my_cols, :], loc_sem.at[2]
        )
    )
    local.append(
        pltpu.make_async_copy(
            w_out.at[span(xl * 768, 768), :], wo.at[:, my_cols], loc_sem.at[3]
        )
    )
    for copy in local:
        copy.start()

    barrier = pltpu.get_barrier_semaphore()
    for dev in (partner, other, zup, zdown, yup, ydown, sibling):
        pl.semaphore_signal(barrier, inc=1, device_id=dev, device_id_type=MESH)
    pl.semaphore_wait(barrier, 7)

    def gather_x0(a):
        there = acts.at[a, my_rows, my_cols]
        send(ins[a], there, ag_send.at[a, 0], ag_recv.at[a, 0], partner).start()
        send(ins[a], there, ag_send.at[a, 1], ag_recv.at[a, 1], other).start()

    def gather_x1(a):
        piece = acts.at[a, my_rows, its_cols]
        arrived(piece, ag_send.at[a, 0], ag_recv.at[a, 0])
        send(piece, piece, ag_send.at[a, 2], ag_recv.at[a, 2], other).start()

    def block(a, j):
        return acts.at[a, chunk(c * 4 + (y + j) % 4), :]

    def theirs(a, j):
        return acts.at[a, chunk((1 - c) * 4 + (y + j) % 4), :]

    def half(a, j, h):
        start = (c * 4 + (y + j) % 4) * CHUNK + 64 * h
        return acts.at[a, span(start, 64, 64), :]

    def to_sibling(a, j, slot):
        blk = block(a, j)
        send(blk, blk, ag_send.at[a, slot], ag_recv.at[a, slot], sibling).start()

    def gather_y0(a):
        local[a].wait()
        its_rows = span(((c * 4 + y) * 2 + 1 - xh) * 64, 64, 64)
        arrived(acts.at[a, its_rows, its_cols], ag_send.at[a, 1], ag_recv.at[a, 1])
        arrived(acts.at[a, its_rows, my_cols], ag_send.at[a, 2], ag_recv.at[a, 2])
        blk = block(a, 0)
        send(blk, blk, ag_send.at[a, 3], ag_recv.at[a, 3], yup).start()
        send(blk, blk, ag_send.at[a, 4], ag_recv.at[a, 4], ydown).start()
        to_sibling(a, 0, 7)

    def gather_y1(a):
        arrived(block(a, 3), ag_send.at[a, 3], ag_recv.at[a, 3])
        part = half(a, 3, 0)
        send(part, part, ag_send.at[a, 5], ag_recv.at[a, 5], yup).start()
        arrived(block(a, 1), ag_send.at[a, 4], ag_recv.at[a, 4])
        part = half(a, 1, 1)
        send(part, part, ag_send.at[a, 6], ag_recv.at[a, 6], ydown).start()
        to_sibling(a, 3, 8)
        to_sibling(a, 1, 9)

    def gather_y2(a):
        arrived(half(a, 2, 0), ag_send.at[a, 5], ag_recv.at[a, 5])
        arrived(half(a, 2, 1), ag_send.at[a, 6], ag_recv.at[a, 6])
        to_sibling(a, 2, 10)

    def gather_end(a):
        for slot, j in ((7, 0), (8, 3), (9, 1), (10, 2)):
            arrived(theirs(a, j), ag_send.at[a, slot], ag_recv.at[a, slot])

    def swap_in(g):
        src = w_in.at[:, span((1 - xl) * 768 + g * GROUP, GROUP)]
        dst = wi.at[my_cols, pl.ds(g * GROUP, GROUP)]
        return send(src, dst, w_send.at[0, g], w_recv.at[0, g], partner)

    def swap_out(g):
        src = w_out.at[span((1 - xl) * 768 + g * GROUP, GROUP), :]
        dst = wo.at[pl.ds(g * GROUP, GROUP), my_cols]
        return send(src, dst, w_send.at[1, g], w_recv.at[1, g], partner)

    def group(g):
        return span(g * GROUP, GROUP, GROUP)

    def term(p, g, k):
        if p == 0:
            return dot(acts[0, chunk(k), :], wi[:, group(g)])
        return dot(acts[1, chunk(k), :], wo[group(g), :], 1, 1)

    def each_group(body):
        def step(g, carry):
            body(g)
            return carry

        lax.fori_loop(0, GROUPS, step, 0)

    def reduce_step(p, s):
        up, down = STEPS[p]

        def body(g):
            if s == 0:
                w_arrived(p, g)
            for way, steps, dev in ((0, up, zup), (1, down, zdown)):
                if s >= steps:
                    continue
                slot = s if way == 0 else up + s
                k = (z + up - s) % 8 if way == 0 else (z + 8 - down + s) % 8
                total = term(p, g, k)
                if s > 0:
                    got = zrecv.at[p, g, slot - 1]
                    arrived(got, rs_send.at[p, g, slot - 1], rs_recv.at[p, g, slot - 1])
                    total = total + got[...].astype(F32)
                zsend[p, g, slot] = total.astype(BF)
                send(
                    zsend.at[p, g, slot],
                    zrecv.at[p, g, slot],
                    rs_send.at[p, g, slot],
                    rs_recv.at[p, g, slot],
                    dev,
                ).start()

        each_group(body)

    def w_arrived(p, g):
        if p == 0:
            ref = wi.at[its_cols, group(g)]
        else:
            ref = wo.at[group(g), its_cols]
        arrived(ref, w_send.at[p, g], w_recv.at[p, g])

    def share(p, g, k):
        return hid.at[p, chunk(k), group(g)]

    def hand_on(p, g, k, slot, dev):
        ref = share(p, g, k)
        send(ref, ref, za_send.at[p, g, slot], za_recv.at[p, g, slot], dev).start()

    def reduce_end(p):
        up, down = STEPS[p]

        def body(g):
            total = term(p, g, z)
            for slot in (up - 1, 6):
                got = zrecv.at[p, g, slot]
                arrived(got, rs_send.at[p, g, slot], rs_recv.at[p, g, slot])
                total = total + got[...].astype(F32)
            if p == 0:
                hid[0, chunk(z), group(g)] = gelu_value(total).astype(BF)
                slope[:, group(g)] = gelu_slope(total)
            else:
                hid[1, chunk(z), group(g)] = (total * slope[:, group(g)]).astype(BF)
            hand_on(p, g, z, 0, zup)
            hand_on(p, g, z, up, zdown)

        each_group(body)

    def gather_step(p, s):
        up, down = STEPS[p]

        def body(g):
            for way, steps, dev in ((0, up, zup), (1, down, zdown)):
                if s > steps:
                    continue
                slot = s if way == 0 else up + s
                k = (z + 8 - s) % 8 if way == 0 else (z + s) % 8
                ref = share(p, g, k)
                arrived(ref, za_send.at[p, g, slot - 1], za_recv.at[p, g, slot - 1])
                if s < steps:
                    hand_on(p, g, k, slot, dev)

        each_group(body)

    def out_terms(p):
        def step(k, carry):
            if p == 0:
                outp[0, chunk(k), :] = dot(hid[0, chunk(k), :], wo[...])
            else:
                outp[1, chunk(k), :] = dot(hid[1, chunk(k), :], wi[...], 1, 1)
            return carry

        lax.fori_loop(0, 8, step, 0)

    def plane_core(p):
        send(
            outp.at[p, span((1 - c) * 512, 512), :],
            crecv.at[p],
            pl_send.at[p, 0],
            pl_recv.at[p, 0],
            sibling,
        ).start()

    def own_sum(p, j, h=None):
        q = (y + j) % 4
        start, size, at = c * 512 + q * 128, 128, q * 128
        if h is not None:
            start, size, at = start + 64 * h, 64, at + 64 * h
        return outp[p, span(start, size, 64), :] + crecv[p, span(at, size, 64), :]

    def plane_y0(p):
        arrived(crecv.at[p], pl_send.at[p, 0], pl_recv.at[p, 0])
        for h, dev in ((0, yup), (1, ydown)):
            ysend0[p, h] = own_sum(p, 2, h).astype(BF)
            send(
                ysend0.at[p, h],
                yrecv0.at[p, h],
                pl_send.at[p, 1 + h],
                pl_recv.at[p, 1 + h],
                dev,
            ).start()

    def plane_y1(p):
        for h, dev, j in ((0, yup, 1), (1, ydown, 3)):
            arrived(yrecv0.at[p, h], pl_send.at[p, 1 + h], pl_recv.at[p, 1 + h])
            got = yrecv0[p, h].astype(F32)
            ysend1[p, h, pl.ds(64 * h, 64), :] = (own_sum(p, j, h) + got).astype(BF)
            ysend1[p, h, pl.ds(64 - 64 * h, 64), :] = own_sum(p, j, 1 - h).astype(BF)
            send(
                ysend1.at[p, h],
                yrecv1.at[p, h],
                pl_send.at[p, 3 + h],
                pl_recv.at[p, 3 + h],
                dev,
            ).start()

    def piece(p, dh, dl):
        rows = span(((xh + dh) % 2) * 64, 64, 64)
        return ysum[p, rows, span(((xl + dl) % 2) * 384, 384)]

    def plane_send(p, m, value, dev):
        xsend[p, m] = value
        send(
            xsend.at[p, m],
            xrecv.at[p, m],
            pl_send.at[p, 5 + m],
            pl_recv.at[p, 5 + m],
            dev,
        ).start()

    def plane_x0(p):
        total = own_sum(p, 0)
        for h in (0, 1):
            arrived(yrecv1.at[p, h], pl_send.at[p, 3 + h], pl_recv.at[p, 3 + h])
            total = total + yrecv1[p, h].astype(F32)
        ysum[p] = total
        plane_send(p, 0, piece(p, 1, 0), other)
        plane_send(p, 1, piece(p, 1, 1), other)

    def x_arrived(p, m):
        arrived(xrecv.at[p, m], pl_send.at[p, 5 + m], pl_recv.at[p, 5 + m])
        return xrecv[p, m]

    def plane_x1(p):
        plane_send(p, 2, piece(p, 0, 1) + x_arrived(p, 0), partner)

    def plane_end(p):
        total = piece(p, 0, 0) + x_arrived(p, 1) + x_arrived(p, 2)
        (o_block, o_gin)[p][...] = total.astype(BF)

    def grad_out(g):
        value = dot(hid[0, :, group(g)], acts[1], 0, 0)
        gw[0, group(g), :] = value.astype(BF)
        there = o_gwout.at[span(xl * 768 + g * GROUP, GROUP), :]
        pltpu.make_async_copy(
            gw.at[0, group(g), my_cols], there, gw_loc.at[0, g]
        ).start()
        send(
            gw.at[0, group(g), its_cols],
            there,
            gw_send.at[0, g],
            gw_recv.at[0, g],
            partner,
        ).start()

    def grad_in(g):
        value = dot(acts[0], hid[1, :, group(g)], 0, 0)
        gw[1, :, group(g)] = value.astype(BF)
        there = o_gwin.at[:, span(xl * 768 + g * GROUP, GROUP)]
        pltpu.make_async_copy(
            gw.at[1, my_cols, group(g)], there, gw_loc.at[1, g]
        ).start()
        send(
            gw.at[1, its_cols, group(g)],
            there,
            gw_send.at[1, g],
            gw_recv.at[1, g],
            partner,
        ).start()

    def grads_end():
        def body(g):
            ref = gw.at[0, group(g), its_cols]
            here = o_gwout.at[span((1 - xl) * 768 + g * GROUP, GROUP), :]
            pltpu.make_async_copy(ref, here, gw_loc.at[0, g]).wait()
            left_here(ref, gw_send.at[0, g], gw_recv.at[0, g])
            arrived(here, gw_send.at[0, g], gw_recv.at[0, g])
            ref = gw.at[1, its_cols, group(g)]
            here = o_gwin.at[:, span((1 - xl) * 768 + g * GROUP, GROUP)]
            pltpu.make_async_copy(ref, here, gw_loc.at[1, g]).wait()
            left_here(ref, gw_send.at[1, g], gw_recv.at[1, g])
            arrived(here, gw_send.at[1, g], gw_recv.at[1, g])

        each_group(body)

    def sends_end():
        for a in (0, 1):
            piece_ref = acts.at[a, my_rows, my_cols]
            for slot in (0, 1, 2):
                left_here(piece_ref, ag_send.at[a, slot], ag_recv.at[a, slot])
            for slot in (3, 4, 7, 8, 9, 10):
                left_here(block(a, 0), ag_send.at[a, slot], ag_recv.at[a, slot])
            for slot in (5, 6):
                left_here(half(a, 0, 0), ag_send.at[a, slot], ag_recv.at[a, slot])

        def body(g):
            left_here(wi.at[my_cols, group(g)], w_send.at[0, g], w_recv.at[0, g])
            left_here(wo.at[group(g), my_cols], w_send.at[1, g], w_recv.at[1, g])
            for p in (0, 1):
                for slot in range(7):
                    ref = zsend.at[p, g, slot]
                    left_here(ref, rs_send.at[p, g, slot], rs_recv.at[p, g, slot])
                    ref = share(p, g, z)
                    left_here(ref, za_send.at[p, g, slot], za_recv.at[p, g, slot])

        each_group(body)
        for p in (0, 1):
            left_here(crecv.at[p], pl_send.at[p, 0], pl_recv.at[p, 0])
            for h in (0, 1):
                left_here(ysend0.at[p, h], pl_send.at[p, 1 + h], pl_recv.at[p, 1 + h])
                left_here(ysend1.at[p, h], pl_send.at[p, 3 + h], pl_recv.at[p, 3 + h])
            for m in (0, 1, 2):
                left_here(xsend.at[p, m], pl_send.at[p, 5 + m], pl_recv.at[p, 5 + m])

    gather_x0(0)
    for g in range(GROUPS):
        swap_in(g).start()
    gather_x1(0)
    gather_y0(0)
    gather_x0(1)
    gather_y1(0)
    gather_x1(1)
    for g in range(GROUPS):
        swap_out(g).start()
    gather_y2(0)
    gather_y0(1)
    gather_end(0)
    local[2].wait()
    reduce_step(0, 0)
    gather_y1(1)
    reduce_step(0, 1)
    gather_y2(1)
    reduce_step(0, 2)
    gather_end(1)
    reduce_step(0, 3)
    local[3].wait()
    reduce_step(1, 0)
    reduce_end(0)
    reduce_step(1, 1)
    gather_step(0, 1)
    reduce_step(1, 2)
    gather_step(0, 2)
    reduce_step(1, 3)
    gather_step(0, 3)
    reduce_end(1)
    gather_step(0, 4)
    gather_step(1, 1)
    out_terms(0)
    plane_core(0)
    grad_out(0)
    gather_step(1, 2)
    plane_y0(0)
    grad_out(1)
    plane_y1(0)
    gather_step(1, 3)
    grad_out(2)
    plane_x0(0)
    gather_step(1, 4)
    out_terms(1)
    plane_core(1)
    plane_x1(0)
    grad_in(0)
    plane_y0(1)
    grad_in(1)
    plane_y1(1)
    grad_in(2)
    plane_x0(1)
    plane_end(0)
    plane_x1(1)
    sends_end()
    plane_end(1)
    grads_end()


def shards(normed, w_in, w_out, cotangent):
    hbm = pl.BlockSpec(memory_space=pl.ANY)
    vmem = pl.BlockSpec(memory_space=pltpu.VMEM)
    dma = pltpu.SemaphoreType.DMA
    return pl.pallas_call(
        kernel,
        out_shape=(
            jax.ShapeDtypeStruct((64, 384), BF),
            jax.ShapeDtypeStruct((64, 384), BF),
            jax.ShapeDtypeStruct((384, 1536), BF),
            jax.ShapeDtypeStruct((1536, 384), BF),
        ),
        in_specs=[hbm] * 4,
        out_specs=(vmem, vmem, hbm, hbm),
        scratch_shapes=[
            pltpu.VMEM((2, TOK, DEPTH), BF),
            pltpu.VMEM((DEPTH, UNITS), BF),
            pltpu.VMEM((UNITS, DEPTH), BF),
            pltpu.VMEM((2, TOK, UNITS), BF),
            pltpu.VMEM((CHUNK, UNITS), F32),
            pltpu.VMEM((2, GROUPS, 7, CHUNK, GROUP), BF),
            pltpu.VMEM((2, GROUPS, 7, CHUNK, GROUP), BF),
            pltpu.VMEM((2, TOK, DEPTH), F32),
            pltpu.VMEM((2, 512, DEPTH), F32),
            pltpu.VMEM((2, 2, 64, DEPTH), BF),
            pltpu.VMEM((2, 2, 64, DEPTH), BF),
            pltpu.VMEM((2, 2, CHUNK, DEPTH), BF),
            pltpu.VMEM((2, 2, CHUNK, DEPTH), BF),
            pltpu.VMEM((2, CHUNK, DEPTH), F32),
            pltpu.VMEM((2, 3, 64, 384), F32),
            pltpu.VMEM((2, 3, 64, 384), F32),
            pltpu.VMEM((2, DEPTH, UNITS), BF),
            dma((4,)),
            dma((2, 11)),
            dma((2, 11)),
            dma((2, GROUPS)),
            dma((2, GROUPS)),
            dma((2, GROUPS, 7)),
            dma((2, GROUPS, 7)),
            dma((2, GROUPS, 7)),
            dma((2, GROUPS, 7)),
            dma((2, 8)),
            dma((2, 8)),
            dma((2, GROUPS)),
            dma((2, GROUPS)),
            dma((2, GROUPS)),
        ],
        compiler_params=pltpu.CompilerParams(
            collective_id=0,
            has_side_effects=True,
            vmem_limit_bytes=50 * 1024 * 1024,
        ),
        cost_estimate=pl.CostEstimate(
            flops=7_247_757_312, bytes_accessed=5_000_000, transcendentals=400_000
        ),
    )(normed, w_in, w_out, cotangent)


def solution(mesh):
    return jax.shard_map(
        shards,
        mesh=mesh,
        in_specs=(
            P(("gy", "gz"), "gx"),
            P("gx", ("gz", "gy")),
            P(("gz", "gy"), "gx"),
            P(("gy", "gz"), "gx"),
        ),
        out_specs=(
            P(("gy", "gz"), "gx"),
            P(("gy", "gz"), "gx"),
            P("gx", ("gz", "gy")),
            P(("gz", "gy"), "gx"),
        ),
        check_vma=False,
    )
```

```python
import math

import jax
import jax.numpy as jnp
from jax import lax
from jax.experimental import pallas as pl
from jax.experimental.pallas import tpu as pltpu
from jax.sharding import PartitionSpec as P

BF = jnp.bfloat16
F32 = jnp.float32
MESH = pl.DeviceIdType.MESH

TOK = 1024
CHUNK = 128
DEPTH = 768
UNITS = 768
GROUP = 256
GROUPS = 3
STEPS = ((4, 3), (3, 4))
PLACE = (7, 6, 4, 2, 0, 1, 3, 5)


def gelu_value(v):
    return 0.5 * v * (1.0 + lax.erf(v / math.sqrt(2.0)))


def gelu_slope(v):
    return 0.5 * (1.0 + lax.erf(v / math.sqrt(2.0))) + v * jnp.exp(
        -0.5 * v * v
    ) / math.sqrt(2.0 * math.pi)


def dot(left, right, ldim=1, rdim=0):
    return lax.dot_general(
        left, right, (((ldim,), (rdim,)), ((), ())), preferred_element_type=F32
    )


def kernel(
    normed,
    w_in,
    w_out,
    cot,
    o_block,
    o_gin,
    o_gwin,
    o_gwout,
    acts,
    wi,
    wo,
    hid,
    slope,
    zsend,
    zrecv,
    outp,
    crecv,
    ysend,
    yrecv,
    ysum,
    xrecv,
    gw,
    loc_sem,
    wl_sem,
    ag_send,
    ag_recv,
    w_send,
    w_recv,
    rs_send,
    rs_recv,
    za_send,
    za_recv,
    pl_send,
    pl_recv,
    gw_loc,
    gw_send,
    gw_recv,
):
    gx, gy, gz = lax.axis_index("gx"), lax.axis_index("gy"), lax.axis_index("gz")
    xl, z, xh, y, c = gx // 8, gx % 8, gy, gz // 2, gz % 2
    cy = c * 4 + y
    partner = ((1 - xl) * 8 + z, xh, gz)
    other = ((1 - xl) * 8 + z, 1 - xh, gz)
    opposite = (gx, 1 - xh, gz)
    zup = (xl * 8 + (z + 1) % 8, xh, gz)
    zdown = (xl * 8 + (z + 7) % 8, xh, gz)
    ynext = [(gx, xh, ((y + d) % 4) * 2 + c) for d in (1, 2, 3)]
    sibling = (gx, xh, y * 2 + 1 - c)

    def send(src, dst, ssem, rsem, dev):
        return pltpu.make_async_remote_copy(
            src_ref=src,
            dst_ref=dst,
            send_sem=ssem,
            recv_sem=rsem,
            device_id=dev,
            device_id_type=MESH,
        )

    def arrived(ref, ssem, rsem):
        send(ref, ref, ssem, rsem, sibling).wait_recv()

    def left_here(ref, ssem, rsem):
        send(ref, ref, ssem, rsem, sibling).wait_send()

    def span(start, size, unit=128):
        return pl.ds(pl.multiple_of(start, unit), size)

    def group(g):
        return pl.ds(g * GROUP, GROUP)

    ins = (normed, cot)
    my_cols = span(xl * 384, 384)
    its_cols = span((1 - xl) * 384, 384)

    def mine(t):
        b = (z + t + xh) % 2
        return b, span(((z + 4 - t + b * (2 * t + 1)) % 8) // 2 * 16, 16, 16)

    def local_piece(a, t):
        b, rows = mine(t)
        there = acts.at[a, 2 * t + b, cy, :, my_cols]
        return pltpu.make_async_copy(ins[a].at[rows, :], there, loc_sem.at[a, t])

    local_w = (
        pltpu.make_async_copy(
            w_in.at[:, span(xl * 768, 768)], wi.at[my_cols, :], wl_sem.at[0]
        ),
        pltpu.make_async_copy(
            w_out.at[span(xl * 768, 768), :], wo.at[:, my_cols], wl_sem.at[1]
        ),
    )
    for a in (0, 1):
        for t in range(4):
            local_piece(a, t).start()
        local_w[a].start()

    barrier = pltpu.get_barrier_semaphore()
    for dev in (partner, other, opposite, zup, zdown, *ynext, sibling):
        pl.semaphore_signal(barrier, inc=1, device_id=dev, device_id_type=MESH)
    pl.semaphore_wait(barrier, 9)

    def gather_x(a, t):
        b, rows = mine(t)
        there = acts.at[a, 2 * t + b, cy, :, my_cols]
        for m, dev in enumerate((partner, other, opposite)):
            sems = ag_send.at[a, t, m], ag_recv.at[a, t, m]
            send(ins[a].at[rows, :], there, *sems, dev).start()

    def gather_y(a, t):
        b, _ = mine(t)
        local_piece(a, t).wait()
        for m, (q, cols) in enumerate(
            ((b, its_cols), (1 - b, its_cols), (1 - b, my_cols))
        ):
            ref = acts.at[a, 2 * t + q, cy, :, cols]
            arrived(ref, ag_send.at[a, t, m], ag_recv.at[a, t, m])
        ref = acts.at[a, pl.ds(2 * t, 2), cy]
        for d in (0, 2, 1):
            sems = ag_send.at[a, t, 3 + d], ag_recv.at[a, t, 3 + d]
            send(ref, ref, *sems, ynext[d]).start()

    def gather_core(a, t):
        for d in range(3):
            ref = acts.at[a, pl.ds(2 * t, 2), c * 4 + (y + 3 - d) % 4]
            arrived(ref, ag_send.at[a, t, 3 + d], ag_recv.at[a, t, 3 + d])
        ref = acts.at[a, pl.ds(2 * t, 2), pl.ds(c * 4, 4)]
        send(ref, ref, ag_send.at[a, t, 6], ag_recv.at[a, t, 6], sibling).start()

    def gathered(a, t):
        ref = acts.at[a, pl.ds(2 * t, 2), pl.ds((1 - c) * 4, 4)]
        arrived(ref, ag_send.at[a, t, 6], ag_recv.at[a, t, 6])

    def swap_in(g):
        src = w_in.at[:, span((1 - xl) * 768 + g * GROUP, GROUP)]
        dst = wi.at[my_cols, group(g)]
        return send(src, dst, w_send.at[0, g], w_recv.at[0, g], partner)

    def swap_out(g):
        src = w_out.at[span((1 - xl) * 768 + g * GROUP, GROUP), :]
        dst = wo.at[group(g), my_cols]
        return send(src, dst, w_send.at[1, g], w_recv.at[1, g], partner)

    def w_arrived(p, g):
        if p == 0:
            ref = wi.at[its_cols, group(g)]
        else:
            ref = wo.at[group(g), its_cols]
        arrived(ref, w_send.at[p, g], w_recv.at[p, g])

    def term(p, g, slot):
        rows = acts[p, PLACE[slot]].reshape(CHUNK, DEPTH)
        if p == 0:
            return dot(rows, wi[:, group(g)])
        return dot(rows, wo[group(g), :], 1, 1)

    def ways(p):
        up, down = STEPS[p]
        return ((up, 0, zup, 1), (down, up, zdown, -1))

    def reduce_step(p, g, s):
        for steps, first, dev, way in ways(p):
            if s >= steps:
                continue
            n = first + s
            total = term(p, g, way * (steps - s) % 8)
            if s > 0:
                got = zrecv.at[p, g, n - 1]
                sems = rs_send.at[p, g, n - 1], rs_recv.at[p, g, n - 1]
                arrived(got, *sems)
                left_here(got, *sems)
                total = total + got[...].astype(F32)
            zsend[p, g, n] = total.astype(BF)
            sems = rs_send.at[p, g, n], rs_recv.at[p, g, n]
            send(zsend.at[p, g, n], zrecv.at[p, g, n], *sems, dev).start()

    def share(p, g, slot):
        return hid.at[p, PLACE[slot % 8], :, group(g)]

    def reduce_end(p, g):
        total = term(p, g, 0)
        for steps, first, _, _ in ways(p):
            n = first + steps - 1
            got = zrecv.at[p, g, n]
            sems = rs_send.at[p, g, n], rs_recv.at[p, g, n]
            arrived(got, *sems)
            left_here(got, *sems)
            total = total + got[...].astype(F32)
        if p == 0:
            hid[0, PLACE[0], :, group(g)] = gelu_value(total).astype(BF)
            slope[:, group(g)] = gelu_slope(total)
        else:
            value = (total * slope[:, group(g)]).astype(BF)
            hid[1, PLACE[0], :, group(g)] = value
        gather_step(p, g, 0)

    def gather_step(p, g, s):
        for steps, first, dev, way in ways(p):
            if s > steps:
                continue
            n = first + s
            ref = share(p, g, -way * s)
            if s > 0:
                sems = za_send.at[p, g, n - 1], za_recv.at[p, g, n - 1]
                arrived(ref, *sems)
                left_here(ref, *sems)
            if s < steps:
                sems = za_send.at[p, g, n], za_recv.at[p, g, n]
                send(ref, share(p, g, -way * (s + 1)), *sems, dev).start()

    done = {}

    def steps(order):
        for u in order:
            p, g = u // 3, u % 3
            s = done[u] = done.get(u, -1) + 1
            if s == 0:
                w_arrived(p, g)
            if s < 4:
                reduce_step(p, g, s)
            elif s == 4:
                reduce_end(p, g)
            else:
                gather_step(p, g, s - 4)

    def plane_core(p, t):
        rows = hid[p, pl.ds(2 * t, 2)].reshape(2 * CHUNK, UNITS)
        if p == 0:
            value = dot(rows, wo[...])
        else:
            value = dot(rows, wi[...], 1, 1)
        outp[p, t] = value.reshape(2, 8, 16, DEPTH)
        src = outp.at[p, t, :, pl.ds((1 - c) * 4, 4)]
        sems = pl_send.at[p, t, 0], pl_recv.at[p, t, 0]
        send(src, crecv.at[p, t], *sems, sibling).start()

    def plane_y(p, t):
        sems = pl_send.at[p, t, 0], pl_recv.at[p, t, 0]
        arrived(crecv.at[p, t], *sems)
        for d in (0, 2, 1):
            at = (y + 1 + d) % 4
            value = outp[p, t, :, c * 4 + at] + crecv[p, t, :, at]
            ysend[p, t, d] = value.astype(BF)
            sems = pl_send.at[p, t, 1 + d], pl_recv.at[p, t, 1 + d]
            send(ysend.at[p, t, d], yrecv.at[p, t, d], *sems, ynext[d]).start()

    def plane_x(p, t):
        total = outp[p, t, :, cy] + crecv[p, t, :, y]
        for d in range(3):
            sems = pl_send.at[p, t, 1 + d], pl_recv.at[p, t, 1 + d]
            arrived(yrecv.at[p, t, d], *sems)
            total = total + yrecv[p, t, d].astype(F32)
        ysum[p, t] = total
        b, _ = mine(t)
        for m, (q, cols, dev) in enumerate(
            (
                (b, its_cols, partner),
                (1 - b, its_cols, other),
                (1 - b, my_cols, opposite),
            )
        ):
            sems = pl_send.at[p, t, 4 + m], pl_recv.at[p, t, 4 + m]
            src = ysum.at[p, t, q, :, cols]
            send(src, xrecv.at[p, t, m], *sems, dev).start()

    def plane_end(p, t):
        b, rows = mine(t)
        total = ysum[p, t, b, :, my_cols]
        for m in range(3):
            sems = pl_send.at[p, t, 4 + m], pl_recv.at[p, t, 4 + m]
            arrived(xrecv.at[p, t, m], *sems)
            total = total + xrecv[p, t, m]
        (o_block, o_gin)[p][rows, :] = total.astype(BF)

    def grad_out(g):
        left = hid[0, :, :, group(g)].reshape(TOK, GROUP)
        value = dot(left, acts[1].reshape(TOK, DEPTH), 0, 0)
        gw[0, group(g), :] = value.astype(BF)
        there = o_gwout.at[span(xl * 768 + g * GROUP, GROUP), :]
        src = gw.at[0, group(g), its_cols]
        send(src, there, gw_send.at[0, g], gw_recv.at[0, g], partner).start()
        src = gw.at[0, group(g), my_cols]
        pltpu.make_async_copy(src, there, gw_loc.at[0, g]).start()

    def grad_in(g):
        right = hid[1, :, :, group(g)].reshape(TOK, GROUP)
        value = dot(acts[0].reshape(TOK, DEPTH), right, 0, 0)
        gw[1, :, group(g)] = value.astype(BF)
        there = o_gwin.at[:, span(xl * 768 + g * GROUP, GROUP)]
        src = gw.at[1, its_cols, group(g)]
        send(src, there, gw_send.at[1, g], gw_recv.at[1, g], partner).start()
        src = gw.at[1, my_cols, group(g)]
        pltpu.make_async_copy(src, there, gw_loc.at[1, g]).start()

    def grads_end():
        for g in range(GROUPS):
            ref = gw.at[0, group(g), its_cols]
            here = o_gwout.at[span((1 - xl) * 768 + g * GROUP, GROUP), :]
            pltpu.make_async_copy(ref, here, gw_loc.at[0, g]).wait()
            left_here(ref, gw_send.at[0, g], gw_recv.at[0, g])
            arrived(here, gw_send.at[0, g], gw_recv.at[0, g])
            ref = gw.at[1, its_cols, group(g)]
            here = o_gwin.at[:, span((1 - xl) * 768 + g * GROUP, GROUP)]
            pltpu.make_async_copy(ref, here, gw_loc.at[1, g]).wait()
            left_here(ref, gw_send.at[1, g], gw_recv.at[1, g])
            arrived(here, gw_send.at[1, g], gw_recv.at[1, g])

    def inputs_left(a):
        for t in range(4):
            for m in range(3):
                ref = acts.at[a, 0, 0, :, pl.ds(0, 384)]
                left_here(ref, ag_send.at[a, t, m], ag_recv.at[a, t, m])
                ref = acts.at[a, pl.ds(0, 2), 0]
                left_here(ref, ag_send.at[a, t, 3 + m], ag_recv.at[a, t, 3 + m])
            ref = acts.at[a, pl.ds(0, 2), pl.ds(0, 4)]
            left_here(ref, ag_send.at[a, t, 6], ag_recv.at[a, t, 6])

    def weights_left():
        for g in range(GROUPS):
            left_here(wi.at[my_cols, group(g)], w_send.at[0, g], w_recv.at[0, g])
            left_here(wo.at[group(g), my_cols], w_send.at[1, g], w_recv.at[1, g])

    def plane_left(p):
        for t in range(4):
            left_here(crecv.at[p, t], pl_send.at[p, t, 0], pl_recv.at[p, t, 0])
            for d in range(3):
                sems = pl_send.at[p, t, 1 + d], pl_recv.at[p, t, 1 + d]
                left_here(ysend.at[p, t, d], *sems)
                sems = pl_send.at[p, t, 4 + d], pl_recv.at[p, t, 4 + d]
                left_here(xrecv.at[p, t, d], *sems)

    for t in range(4):
        gather_x(0, t)
    swap_in(0).start()
    for t in range(4):
        gather_x(1, t)
    for g in (1, 2):
        swap_in(g).start()
    for g in range(GROUPS):
        swap_out(g).start()
    for t in range(4):
        gather_y(0, t)
    gather_core(0, 0)
    for t in range(4):
        gather_y(1, t)
    local_w[0].wait()
    gather_core(0, 1)
    gathered(0, 0)
    steps((0, 1))
    gather_core(0, 2)
    gathered(0, 1)
    steps((0, 1, 2))
    gather_core(0, 3)
    gathered(0, 2)
    steps((0, 1, 2))
    gather_core(1, 0)
    gather_core(1, 1)
    gathered(0, 3)
    steps((0, 1))
    gather_core(1, 2)
    gather_core(1, 3)
    for t in range(4):
        gathered(1, t)
    local_w[1].wait()
    steps((3, 4, 2, 3, 0, 5, 1, 4, 2, 3, 0, 5, 1, 3, 4, 2, 0, 3, 5, 4, 1, 2, 0))
    inputs_left(0)
    steps((5, 3, 4, 1, 2, 5, 0))
    grad_out(0)
    steps((3, 4, 1))
    grad_out(1)
    steps((2, 5))
    plane_core(0, 3)
    steps((3, 4, 2))
    grad_out(2)
    plane_core(0, 2)
    plane_core(0, 1)
    plane_core(0, 0)
    steps((3,))
    grad_in(0)
    steps((5, 4))
    plane_core(1, 3)
    for t in (3, 2, 1, 0):
        plane_y(0, t)
    plane_core(1, 2)
    steps((5,))
    plane_core(1, 1)
    plane_y(1, 3)
    plane_y(1, 2)
    steps((4,))
    grad_in(1)
    for t in (3, 2, 1, 0):
        plane_x(0, t)
    plane_y(1, 1)
    steps((5,))
    plane_core(1, 0)
    grad_in(2)
    plane_y(1, 0)
    plane_x(1, 3)
    plane_x(1, 2)
    plane_x(1, 1)
    for t in (3, 2, 1, 0):
        plane_end(0, t)
    weights_left()
    inputs_left(1)
    plane_x(1, 0)
    plane_left(0)
    for t in (3, 2, 1, 0):
        plane_end(1, t)
    plane_left(1)
    grads_end()


def shards(normed, w_in, w_out, cotangent):
    hbm = pl.BlockSpec(memory_space=pltpu.HBM)
    vmem = pl.BlockSpec(memory_space=pltpu.VMEM)
    dma = pltpu.SemaphoreType.DMA
    return pl.pallas_call(
        kernel,
        out_shape=(
            jax.ShapeDtypeStruct((64, 384), BF),
            jax.ShapeDtypeStruct((64, 384), BF),
            jax.ShapeDtypeStruct((384, 1536), BF),
            jax.ShapeDtypeStruct((1536, 384), BF),
        ),
        in_specs=[hbm] * 4,
        out_specs=(vmem, vmem, hbm, hbm),
        scratch_shapes=[
            pltpu.VMEM((2, 8, 8, 16, DEPTH), BF),
            pltpu.VMEM((DEPTH, UNITS), BF),
            pltpu.VMEM((UNITS, DEPTH), BF),
            pltpu.VMEM((2, 8, CHUNK, UNITS), BF),
            pltpu.VMEM((CHUNK, UNITS), F32),
            pltpu.VMEM((2, GROUPS, 7, CHUNK, GROUP), BF),
            pltpu.VMEM((2, GROUPS, 7, CHUNK, GROUP), BF),
            pltpu.VMEM((2, 4, 2, 8, 16, DEPTH), F32),
            pltpu.VMEM((2, 4, 2, 4, 16, DEPTH), F32),
            pltpu.VMEM((2, 4, 3, 2, 16, DEPTH), BF),
            pltpu.VMEM((2, 4, 3, 2, 16, DEPTH), BF),
            pltpu.VMEM((2, 4, 2, 16, DEPTH), F32),
            pltpu.VMEM((2, 4, 3, 16, 384), F32),
            pltpu.VMEM((2, DEPTH, UNITS), BF),
            dma((2, 4)),
            dma((2,)),
            dma((2, 4, 7)),
            dma((2, 4, 7)),
            dma((2, GROUPS)),
            dma((2, GROUPS)),
            dma((2, GROUPS, 7)),
            dma((2, GROUPS, 7)),
            dma((2, GROUPS, 7)),
            dma((2, GROUPS, 7)),
            dma((2, 4, 7)),
            dma((2, 4, 7)),
            dma((2, GROUPS)),
            dma((2, GROUPS)),
            dma((2, GROUPS)),
        ],
        compiler_params=pltpu.CompilerParams(
            collective_id=0,
            has_side_effects=True,
            vmem_limit_bytes=58 * 1024 * 1024,
        ),
        cost_estimate=pl.CostEstimate(
            flops=7_247_757_312, bytes_accessed=5_000_000, transcendentals=400_000
        ),
    )(normed, w_in, w_out, cotangent)


def solution(mesh):
    return jax.shard_map(
        shards,
        mesh=mesh,
        in_specs=(
            P(("gy", "gz"), "gx"),
            P("gx", ("gz", "gy")),
            P(("gz", "gy"), "gx"),
            P(("gy", "gz"), "gx"),
        ),
        out_specs=(
            P(("gy", "gz"), "gx"),
            P(("gy", "gz"), "gx"),
            P("gx", ("gz", "gy")),
            P(("gz", "gy"), "gx"),
        ),
        check_vma=False,
    )
```

```python
import math

import jax
import jax.numpy as jnp
from jax import lax
from jax.experimental import pallas as pl
from jax.experimental.pallas import tpu as pltpu
from jax.sharding import PartitionSpec as P

BF = jnp.bfloat16
F32 = jnp.float32
MESH = pl.DeviceIdType.MESH

TOK = 1024
CHUNK = 128
DEPTH = 768
UNITS = 768
GROUP = 256
GROUPS = 3
STEPS = ((4, 3), (3, 4))
PLACE = (7, 6, 4, 2, 0, 1, 3, 5)


SCHEDULE = (
    ("gather_y", 0, 0),
    ("gather_y", 0, 1),
    ("gather_y", 0, 2),
    ("gather_y", 0, 3),
    ("gather_core", 0, 0),
    ("reduce", 0, 0, 0),
    ("gather_y", 1, 0),
    ("gather_core", 0, 1),
    ("gather_y", 1, 1),
    ("gather_y", 1, 2),
    ("gather_y", 1, 3),
    ("gather_core", 0, 2),
    ("reduce", 0, 0, 1),
    ("gather_core", 0, 3),
    ("reduce", 0, 1, 0),
    ("gather_core", 1, 0),
    ("reduce", 0, 0, 2),
    ("gather_core", 1, 1),
    ("reduce", 0, 1, 1),
    ("reduce", 0, 2, 0),
    ("gather_core", 1, 2),
    ("reduce", 0, 0, 3),
    ("gather_core", 1, 3),
    ("reduce", 0, 1, 2),
    ("reduce", 1, 0, 0),
    ("reduce", 0, 2, 1),
    ("reduce", 0, 0, 4),
    ("reduce", 0, 1, 3),
    ("reduce", 1, 1, 0),
    ("reduce", 0, 2, 2),
    ("gather", 0, 0, 1),
    ("reduce", 0, 1, 4),
    ("reduce", 1, 2, 0),
    ("reduce", 0, 2, 3),
    ("gather", 0, 0, 2),
    ("gather", 0, 1, 1),
    ("reduce", 1, 2, 1),
    ("reduce", 0, 2, 4),
    ("gather", 0, 0, 3),
    ("gather", 0, 1, 2),
    ("reduce", 1, 2, 2),
    ("reduce", 1, 1, 1),
    ("gather", 0, 0, 4),
    ("grad", 0, 0),
    ("reduce", 1, 0, 1),
    ("reduce", 1, 2, 3),
    ("gather", 0, 1, 3),
    ("gather", 0, 2, 1),
    ("plane_core", 0, 3),
    ("reduce", 1, 1, 2),
    ("plane_y", 0, 3),
    ("reduce", 1, 2, 4),
    ("gather", 0, 1, 4),
    ("grad", 0, 1),
    ("reduce", 1, 0, 2),
    ("reduce", 1, 1, 3),
    ("gather", 0, 2, 2),
    ("plane_core", 0, 2),
    ("plane_x", 0, 3),
    ("gather", 1, 2, 1),
    ("plane_y", 0, 2),
    ("reduce", 1, 0, 3),
    ("reduce", 1, 1, 4),
    ("gather", 0, 2, 3),
    ("plane_core", 0, 1),
    ("plane_end", 0, 3),
    ("gather", 1, 2, 2),
    ("plane_x", 0, 2),
    ("plane_y", 0, 1),
    ("reduce", 1, 0, 4),
    ("gather", 1, 1, 1),
    ("gather", 0, 2, 4),
    ("grad", 0, 2),
    ("plane_core", 0, 0),
    ("plane_end", 0, 2),
    ("gather", 1, 2, 3),
    ("plane_x", 0, 1),
    ("gather", 1, 0, 1),
    ("plane_core", 1, 3),
    ("plane_y", 0, 0),
    ("gather", 1, 1, 2),
    ("gather", 1, 2, 4),
    ("grad", 1, 2),
    ("plane_y", 1, 3),
    ("gather", 1, 0, 2),
    ("plane_core", 1, 2),
    ("plane_x", 0, 0),
    ("gather", 1, 1, 3),
    ("plane_end", 0, 1),
    ("plane_y", 1, 2),
    ("gather", 1, 0, 3),
    ("plane_core", 1, 1),
    ("plane_x", 1, 3),
    ("gather", 1, 1, 4),
    ("grad", 1, 1),
    ("plane_y", 1, 1),
    ("plane_x", 1, 2),
    ("gather", 1, 0, 4),
    ("plane_end", 0, 0),
    ("plane_core", 1, 0),
    ("grad", 1, 0),
    ("plane_end", 1, 3),
    ("plane_y", 1, 0),
    ("plane_x", 1, 1),
    ("plane_end", 1, 2),
    ("plane_x", 1, 0),
    ("plane_end", 1, 1),
    ("plane_end", 1, 0),
)


def gelu_value(v):
    return 0.5 * v * (1.0 + lax.erf(v / math.sqrt(2.0)))


def gelu_slope(v):
    return 0.5 * (1.0 + lax.erf(v / math.sqrt(2.0))) + v * jnp.exp(
        -0.5 * v * v
    ) / math.sqrt(2.0 * math.pi)


def dot(left, right, ldim=1, rdim=0):
    return lax.dot_general(
        left, right, (((ldim,), (rdim,)), ((), ())), preferred_element_type=F32
    )


def kernel(
    normed,
    w_in,
    w_out,
    cot,
    o_block,
    o_gin,
    o_gwin,
    o_gwout,
    acts,
    wi,
    wo,
    hid,
    slope,
    zsend,
    zrecv,
    outp,
    crecv,
    ysend,
    yrecv,
    ysum,
    xrecv,
    gw,
    loc_sem,
    wl_sem,
    ag_send,
    ag_recv,
    w_send,
    w_recv,
    rs_send,
    rs_recv,
    za_send,
    za_recv,
    pl_send,
    pl_recv,
    gw_loc,
    gw_send,
    gw_recv,
):
    gx, gy, gz = lax.axis_index("gx"), lax.axis_index("gy"), lax.axis_index("gz")
    xl, z, xh, y, c = gx // 8, gx % 8, gy, gz // 2, gz % 2
    cy = c * 4 + y
    partner = ((1 - xl) * 8 + z, xh, gz)
    other = ((1 - xl) * 8 + z, 1 - xh, gz)
    opposite = (gx, 1 - xh, gz)
    zup = (xl * 8 + (z + 1) % 8, xh, gz)
    zdown = (xl * 8 + (z + 7) % 8, xh, gz)
    ynext = [(gx, xh, ((y + d) % 4) * 2 + c) for d in (1, 2, 3)]
    sibling = (gx, xh, y * 2 + 1 - c)

    def send(src, dst, ssem, rsem, dev):
        return pltpu.make_async_remote_copy(
            src_ref=src,
            dst_ref=dst,
            send_sem=ssem,
            recv_sem=rsem,
            device_id=dev,
            device_id_type=MESH,
        )

    def arrived(ref, ssem, rsem):
        send(ref, ref, ssem, rsem, sibling).wait_recv()

    def left_here(ref, ssem, rsem):
        send(ref, ref, ssem, rsem, sibling).wait_send()

    def span(start, size, unit=128):
        return pl.ds(pl.multiple_of(start, unit), size)

    def group(g):
        return pl.ds(g * GROUP, GROUP)

    ins = (normed, cot)
    my_cols = span(xl * 384, 384)
    its_cols = span((1 - xl) * 384, 384)

    def mine(t):
        b = (z + t + xh) % 2
        return b, span(((z + 4 - t + b * (2 * t + 1)) % 8) // 2 * 16, 16, 16)

    def local_piece(a, t):
        b, rows = mine(t)
        there = acts.at[a, 2 * t + b, cy, :, my_cols]
        return pltpu.make_async_copy(ins[a].at[rows, :], there, loc_sem.at[a, t])

    local_w = (
        pltpu.make_async_copy(
            w_in.at[:, span(xl * 768, 768)], wi.at[my_cols, :], wl_sem.at[0]
        ),
        pltpu.make_async_copy(
            w_out.at[span(xl * 768, 768), :], wo.at[:, my_cols], wl_sem.at[1]
        ),
    )
    for a in (0, 1):
        for t in range(4):
            local_piece(a, t).start()
        local_w[a].start()

    barrier = pltpu.get_barrier_semaphore()
    for dev in (partner, other, opposite, zup, zdown, *ynext, sibling):
        pl.semaphore_signal(barrier, inc=1, device_id=dev, device_id_type=MESH)
    pl.semaphore_wait(barrier, 9)

    def gather_x(a, t):
        b, rows = mine(t)
        there = acts.at[a, 2 * t + b, cy, :, my_cols]
        for m, dev in enumerate((partner, other, opposite)):
            sems = ag_send.at[a, t, m], ag_recv.at[a, t, m]
            send(ins[a].at[rows, :], there, *sems, dev).start()

    def gather_y(a, t):
        b, _ = mine(t)
        local_piece(a, t).wait()
        for m, (q, cols) in enumerate(
            ((b, its_cols), (1 - b, its_cols), (1 - b, my_cols))
        ):
            ref = acts.at[a, 2 * t + q, cy, :, cols]
            arrived(ref, ag_send.at[a, t, m], ag_recv.at[a, t, m])
        ref = acts.at[a, pl.ds(2 * t, 2), cy]
        for d in (0, 2, 1):
            sems = ag_send.at[a, t, 3 + d], ag_recv.at[a, t, 3 + d]
            send(ref, ref, *sems, ynext[d]).start()

    def gather_core(a, t):
        for d in range(3):
            ref = acts.at[a, pl.ds(2 * t, 2), c * 4 + (y + 3 - d) % 4]
            arrived(ref, ag_send.at[a, t, 3 + d], ag_recv.at[a, t, 3 + d])
        ref = acts.at[a, pl.ds(2 * t, 2), pl.ds(c * 4, 4)]
        send(ref, ref, ag_send.at[a, t, 6], ag_recv.at[a, t, 6], sibling).start()

    def gathered(a, t):
        ref = acts.at[a, pl.ds(2 * t, 2), pl.ds((1 - c) * 4, 4)]
        arrived(ref, ag_send.at[a, t, 6], ag_recv.at[a, t, 6])

    def swap_in(g):
        src = w_in.at[:, span((1 - xl) * 768 + g * GROUP, GROUP)]
        dst = wi.at[my_cols, group(g)]
        return send(src, dst, w_send.at[0, g], w_recv.at[0, g], partner)

    def swap_out(g):
        src = w_out.at[span((1 - xl) * 768 + g * GROUP, GROUP), :]
        dst = wo.at[group(g), my_cols]
        return send(src, dst, w_send.at[1, g], w_recv.at[1, g], partner)

    def w_arrived(p, g):
        if p == 0:
            ref = wi.at[its_cols, group(g)]
        else:
            ref = wo.at[group(g), its_cols]
        arrived(ref, w_send.at[p, g], w_recv.at[p, g])

    def term(p, g, slot):
        rows = acts[p, PLACE[slot]].reshape(CHUNK, DEPTH)
        if p == 0:
            return dot(rows, wi[:, group(g)])
        return dot(rows, wo[group(g), :], 1, 1)

    def ways(p):
        up, down = STEPS[p]
        return ((up, 0, zup, 1), (down, up, zdown, -1))

    def reduce_step(p, g, s):
        for steps, first, dev, way in ways(p):
            if s >= steps:
                continue
            n = first + s
            total = term(p, g, way * (steps - s) % 8)
            if s > 0:
                got = zrecv.at[p, g, n - 1]
                sems = rs_send.at[p, g, n - 1], rs_recv.at[p, g, n - 1]
                arrived(got, *sems)
                left_here(got, *sems)
                total = total + got[...].astype(F32)
            zsend[p, g, n] = total.astype(BF)
            sems = rs_send.at[p, g, n], rs_recv.at[p, g, n]
            send(zsend.at[p, g, n], zrecv.at[p, g, n], *sems, dev).start()

    def share(p, g, slot):
        return hid.at[p, PLACE[slot % 8], :, group(g)]

    def reduce_end(p, g):
        total = term(p, g, 0)
        for steps, first, _, _ in ways(p):
            n = first + steps - 1
            got = zrecv.at[p, g, n]
            sems = rs_send.at[p, g, n], rs_recv.at[p, g, n]
            arrived(got, *sems)
            left_here(got, *sems)
            total = total + got[...].astype(F32)
        if p == 0:
            hid[0, PLACE[0], :, group(g)] = gelu_value(total).astype(BF)
            slope[:, group(g)] = gelu_slope(total)
        else:
            value = (total * slope[:, group(g)]).astype(BF)
            hid[1, PLACE[0], :, group(g)] = value
        gather_step(p, g, 0)

    def gather_step(p, g, s):
        for steps, first, dev, way in ways(p):
            if s > steps:
                continue
            n = first + s
            ref = share(p, g, -way * s)
            if s > 0:
                sems = za_send.at[p, g, n - 1], za_recv.at[p, g, n - 1]
                arrived(ref, *sems)
                left_here(ref, *sems)
            if s < steps:
                sems = za_send.at[p, g, n], za_recv.at[p, g, n]
                send(ref, share(p, g, -way * (s + 1)), *sems, dev).start()

    here = set()

    def need(p, *slots):
        for slot in slots:
            t = PLACE[slot % 8] // 2
            if (p, t) not in here:
                gathered(p, t)
                here.add((p, t))

    def reduce(p, g, s):
        if s == 0:
            if p not in here:
                local_w[p].wait()
                here.add(p)
            w_arrived(p, g)
        for steps, _, _, way in ways(p):
            if s < steps:
                need(p, way * (steps - s))
        if s < 4:
            reduce_step(p, g, s)
        else:
            need(p, 0)
            reduce_end(p, g)

    def plane_core(p, t):
        rows = hid[p, pl.ds(2 * t, 2)].reshape(2 * CHUNK, UNITS)
        if p == 0:
            value = dot(rows, wo[...])
        else:
            value = dot(rows, wi[...], 1, 1)
        outp[p, t] = value.reshape(2, 8, 16, DEPTH)
        src = outp.at[p, t, :, pl.ds((1 - c) * 4, 4)]
        sems = pl_send.at[p, t, 0], pl_recv.at[p, t, 0]
        send(src, crecv.at[p, t], *sems, sibling).start()

    def plane_y(p, t):
        sems = pl_send.at[p, t, 0], pl_recv.at[p, t, 0]
        arrived(crecv.at[p, t], *sems)
        for d in (0, 2, 1):
            at = (y + 1 + d) % 4
            value = outp[p, t, :, c * 4 + at] + crecv[p, t, :, at]
            ysend[p, t, d] = value.astype(BF)
            sems = pl_send.at[p, t, 1 + d], pl_recv.at[p, t, 1 + d]
            send(ysend.at[p, t, d], yrecv.at[p, t, d], *sems, ynext[d]).start()

    def plane_x(p, t):
        total = outp[p, t, :, cy] + crecv[p, t, :, y]
        for d in range(3):
            sems = pl_send.at[p, t, 1 + d], pl_recv.at[p, t, 1 + d]
            arrived(yrecv.at[p, t, d], *sems)
            total = total + yrecv[p, t, d].astype(F32)
        ysum[p, t] = total
        b, _ = mine(t)
        for m, (q, cols, dev) in enumerate(
            (
                (b, its_cols, partner),
                (1 - b, its_cols, other),
                (1 - b, my_cols, opposite),
            )
        ):
            sems = pl_send.at[p, t, 4 + m], pl_recv.at[p, t, 4 + m]
            src = ysum.at[p, t, q, :, cols]
            send(src, xrecv.at[p, t, m], *sems, dev).start()

    def plane_end(p, t):
        b, rows = mine(t)
        total = ysum[p, t, b, :, my_cols]
        for m in range(3):
            sems = pl_send.at[p, t, 4 + m], pl_recv.at[p, t, 4 + m]
            arrived(xrecv.at[p, t, m], *sems)
            total = total + xrecv[p, t, m]
        (o_block, o_gin)[p][rows, :] = total.astype(BF)

    def grad_out(g):
        left = hid[0, :, :, group(g)].reshape(TOK, GROUP)
        value = dot(left, acts[1].reshape(TOK, DEPTH), 0, 0)
        gw[0, group(g), :] = value.astype(BF)
        there = o_gwout.at[span(xl * 768 + g * GROUP, GROUP), :]
        src = gw.at[0, group(g), its_cols]
        send(src, there, gw_send.at[0, g], gw_recv.at[0, g], partner).start()
        src = gw.at[0, group(g), my_cols]
        pltpu.make_async_copy(src, there, gw_loc.at[0, g]).start()

    def grad_in(g):
        right = hid[1, :, :, group(g)].reshape(TOK, GROUP)
        value = dot(acts[0].reshape(TOK, DEPTH), right, 0, 0)
        gw[1, :, group(g)] = value.astype(BF)
        there = o_gwin.at[:, span(xl * 768 + g * GROUP, GROUP)]
        src = gw.at[1, its_cols, group(g)]
        send(src, there, gw_send.at[1, g], gw_recv.at[1, g], partner).start()
        src = gw.at[1, my_cols, group(g)]
        pltpu.make_async_copy(src, there, gw_loc.at[1, g]).start()

    def grad(p, g):
        need(1 - p, *range(8))
        (grad_out, grad_in)[p](g)

    def grads_end():
        for g in range(GROUPS):
            ref = gw.at[0, group(g), its_cols]
            here = o_gwout.at[span((1 - xl) * 768 + g * GROUP, GROUP), :]
            pltpu.make_async_copy(ref, here, gw_loc.at[0, g]).wait()
            left_here(ref, gw_send.at[0, g], gw_recv.at[0, g])
            arrived(here, gw_send.at[0, g], gw_recv.at[0, g])
            ref = gw.at[1, its_cols, group(g)]
            here = o_gwin.at[:, span((1 - xl) * 768 + g * GROUP, GROUP)]
            pltpu.make_async_copy(ref, here, gw_loc.at[1, g]).wait()
            left_here(ref, gw_send.at[1, g], gw_recv.at[1, g])
            arrived(here, gw_send.at[1, g], gw_recv.at[1, g])

    def inputs_left(a):
        for t in range(4):
            for m in range(3):
                ref = acts.at[a, 0, 0, :, pl.ds(0, 384)]
                left_here(ref, ag_send.at[a, t, m], ag_recv.at[a, t, m])
                ref = acts.at[a, pl.ds(0, 2), 0]
                left_here(ref, ag_send.at[a, t, 3 + m], ag_recv.at[a, t, 3 + m])
            ref = acts.at[a, pl.ds(0, 2), pl.ds(0, 4)]
            left_here(ref, ag_send.at[a, t, 6], ag_recv.at[a, t, 6])

    def weights_left():
        for g in range(GROUPS):
            left_here(wi.at[my_cols, group(g)], w_send.at[0, g], w_recv.at[0, g])
            left_here(wo.at[group(g), my_cols], w_send.at[1, g], w_recv.at[1, g])

    def plane_left(p):
        for t in range(4):
            left_here(crecv.at[p, t], pl_send.at[p, t, 0], pl_recv.at[p, t, 0])
            for d in range(3):
                sems = pl_send.at[p, t, 1 + d], pl_recv.at[p, t, 1 + d]
                left_here(ysend.at[p, t, d], *sems)
                sems = pl_send.at[p, t, 4 + d], pl_recv.at[p, t, 4 + d]
                left_here(xrecv.at[p, t, d], *sems)

    for t in range(4):
        gather_x(0, t)
    swap_in(0).start()
    for t in range(4):
        gather_x(1, t)
    for g in range(1, GROUPS):
        swap_in(g).start()
    for g in range(GROUPS):
        swap_out(g).start()
    table = {
        "gather_y": gather_y,
        "gather_core": gather_core,
        "reduce": reduce,
        "gather": gather_step,
        "grad": grad,
        "plane_core": plane_core,
        "plane_y": plane_y,
        "plane_x": plane_x,
        "plane_end": plane_end,
    }
    for name, *where in SCHEDULE:
        table[name](*where)
    weights_left()
    for a in (0, 1):
        inputs_left(a)
        plane_left(a)
    grads_end()


def settle(*refs):
    ins, outs, held, sems = refs[:4], refs[4:8], refs[8:12], refs[12]
    loads = [pltpu.make_async_copy(ins[i], held[i], sems.at[0, i]) for i in range(4)]
    stores = [pltpu.make_async_copy(held[i], outs[i], sems.at[1, i]) for i in range(4)]
    for i in (2, 3, 0, 1):
        loads[i].start()
    for i in (2, 3, 0, 1):
        loads[i].wait()
        stores[i].start()
    for store in stores:
        store.wait()


def shards(normed, w_in, w_out, cotangent):
    hbm = pl.BlockSpec(memory_space=pltpu.HBM)
    vmem = pl.BlockSpec(memory_space=pltpu.VMEM)
    dma = pltpu.SemaphoreType.DMA
    shapes = (
        jax.ShapeDtypeStruct((64, 384), BF),
        jax.ShapeDtypeStruct((64, 384), BF),
        jax.ShapeDtypeStruct((384, 1536), BF),
        jax.ShapeDtypeStruct((1536, 384), BF),
    )
    results = pl.pallas_call(
        kernel,
        out_shape=shapes,
        in_specs=[hbm] * 4,
        out_specs=(vmem, vmem, hbm, hbm),
        scratch_shapes=[
            pltpu.VMEM((2, 8, 8, 16, DEPTH), BF),
            pltpu.VMEM((DEPTH, UNITS), BF),
            pltpu.VMEM((UNITS, DEPTH), BF),
            pltpu.VMEM((2, 8, CHUNK, UNITS), BF),
            pltpu.VMEM((CHUNK, UNITS), F32),
            pltpu.VMEM((2, GROUPS, 7, CHUNK, GROUP), BF),
            pltpu.VMEM((2, GROUPS, 7, CHUNK, GROUP), BF),
            pltpu.VMEM((2, 4, 2, 8, 16, DEPTH), F32),
            pltpu.VMEM((2, 4, 2, 4, 16, DEPTH), F32),
            pltpu.VMEM((2, 4, 3, 2, 16, DEPTH), BF),
            pltpu.VMEM((2, 4, 3, 2, 16, DEPTH), BF),
            pltpu.VMEM((2, 4, 2, 16, DEPTH), F32),
            pltpu.VMEM((2, 4, 3, 16, 384), F32),
            pltpu.VMEM((2, DEPTH, UNITS), BF),
            dma((2, 4)),
            dma((2,)),
            dma((2, 4, 7)),
            dma((2, 4, 7)),
            dma((2, GROUPS)),
            dma((2, GROUPS)),
            dma((2, GROUPS, 7)),
            dma((2, GROUPS, 7)),
            dma((2, GROUPS, 7)),
            dma((2, GROUPS, 7)),
            dma((2, 4, 7)),
            dma((2, 4, 7)),
            dma((2, GROUPS)),
            dma((2, GROUPS)),
            dma((2, GROUPS)),
        ],
        compiler_params=pltpu.CompilerParams(
            collective_id=0,
            has_side_effects=True,
            vmem_limit_bytes=58 * 1024 * 1024,
        ),
        cost_estimate=pl.CostEstimate(
            flops=7_247_757_312, bytes_accessed=5_000_000, transcendentals=400_000
        ),
    )(normed, w_in, w_out, cotangent)
    return pl.pallas_call(
        settle,
        out_shape=shapes,
        in_specs=[hbm] * 4,
        out_specs=(hbm,) * 4,
        scratch_shapes=[
            *(pltpu.VMEM(shape.shape, BF) for shape in shapes),
            dma((2, 4)),
        ],
        cost_estimate=pl.CostEstimate(
            flops=0, bytes_accessed=4_900_000, transcendentals=0
        ),
    )(*results)


def solution(mesh):
    return jax.shard_map(
        shards,
        mesh=mesh,
        in_specs=(
            P(("gy", "gz"), "gx"),
            P("gx", ("gz", "gy")),
            P(("gz", "gy"), "gx"),
            P(("gy", "gz"), "gx"),
        ),
        out_specs=(
            P(("gy", "gz"), "gx"),
            P(("gy", "gz"), "gx"),
            P("gx", ("gz", "gy")),
            P(("gz", "gy"), "gx"),
        ),
        check_vma=False,
    )
```

```python
import math

import jax
import jax.numpy as jnp
from jax import lax
from jax.experimental import pallas as pl
from jax.experimental.pallas import tpu as pltpu
from jax.sharding import PartitionSpec as P

BF = jnp.bfloat16
F32 = jnp.float32
MESH = pl.DeviceIdType.MESH

TOK = 1024
CHUNK = 128
DEPTH = 768
UNITS = 768
GROUP = 256
GROUPS = 3
STEPS = ((4, 3), (3, 4))
PLACE = (7, 6, 4, 2, 0, 1, 3, 5)
DIRECT = 0


GATHER_Y, GATHER_CORE, REDUCE, GATHER, GRAD = range(5)
PLANE_CORE, PLANE_Y, PLANE_X, PLANE_X1, PLANE_END = range(5, 10)
SCHEDULE = (
    (GATHER_Y, 0, 0),
    (GATHER_Y, 0, 1),
    (GATHER_Y, 0, 2),
    (GATHER_Y, 0, 3),
    (GATHER_CORE, 0, 0),
    (REDUCE, 0, 0, 0),
    (GATHER_Y, 1, 1),
    (GATHER_CORE, 0, 1),
    (REDUCE, 0, 0, 1),
    (GATHER_Y, 1, 0),
    (GATHER_CORE, 0, 2),
    (REDUCE, 0, 1, 0),
    (GATHER_Y, 1, 3),
    (REDUCE, 0, 0, 2),
    (GATHER_CORE, 0, 3),
    (GATHER_CORE, 1, 1),
    (REDUCE, 0, 1, 1),
    (REDUCE, 0, 2, 0),
    (REDUCE, 0, 0, 3),
    (REDUCE, 0, 1, 2),
    (GATHER_Y, 1, 2),
    (REDUCE, 0, 2, 1),
    (GATHER_CORE, 1, 0),
    (REDUCE, 0, 0, 4),
    (GATHER_CORE, 1, 3),
    (REDUCE, 1, 0, 0),
    (REDUCE, 0, 2, 2),
    (GATHER, 0, 0, 1),
    (GATHER_CORE, 1, 2),
    (REDUCE, 0, 1, 3),
    (REDUCE, 1, 1, 0),
    (REDUCE, 0, 2, 3),
    (REDUCE, 1, 2, 0),
    (REDUCE, 0, 1, 4),
    (REDUCE, 0, 2, 4),
    (REDUCE, 1, 0, 1),
    (REDUCE, 1, 2, 1),
    (GATHER, 0, 0, 2),
    (GATHER, 0, 2, 1),
    (GATHER, 0, 1, 1),
    (REDUCE, 1, 2, 2),
    (GATHER, 0, 0, 3),
    (REDUCE, 1, 0, 2),
    (REDUCE, 1, 1, 1),
    (PLANE_CORE, 0, 3, 0),
    (GATHER, 0, 2, 2),
    (REDUCE, 1, 0, 3),
    (GATHER, 0, 1, 2),
    (GATHER, 0, 0, 4),
    (PLANE_CORE, 0, 2, 1),
    (PLANE_Y, 0, 3, 0),
    (PLANE_CORE, 0, 1, 1),
    (PLANE_CORE, 0, 3, 1),
    (GRAD, 0, 0),
    (REDUCE, 1, 1, 2),
    (REDUCE, 1, 0, 4),
    (REDUCE, 1, 2, 3),
    (PLANE_CORE, 0, 2, 0),
    (PLANE_Y, 0, 3, 1),
    (GATHER, 0, 2, 3),
    (PLANE_Y, 0, 2, 0),
    (GATHER, 0, 1, 3),
    (REDUCE, 1, 1, 3),
    (PLANE_Y, 0, 1, 1),
    (PLANE_CORE, 0, 1, 0),
    (GATHER, 1, 0, 1),
    (PLANE_Y, 0, 2, 1),
    (REDUCE, 1, 2, 4),
    (GATHER, 0, 2, 4),
    (GRAD, 0, 2),
    (PLANE_Y, 0, 1, 0),
    (GATHER, 0, 1, 4),
    (REDUCE, 1, 1, 4),
    (PLANE_CORE, 0, 0, 1),
    (GRAD, 0, 1),
    (GATHER, 1, 0, 2),
    (PLANE_X, 0, 3),
    (PLANE_CORE, 0, 0, 0),
    (GATHER, 1, 2, 1),
    (PLANE_Y, 0, 0, 1),
    (PLANE_Y, 0, 0, 0),
    (GATHER, 1, 1, 1),
    (PLANE_CORE, 1, 3, 1),
    (PLANE_X, 0, 2),
    (PLANE_X, 0, 1),
    (PLANE_CORE, 1, 3, 0),
    (GATHER, 1, 0, 3),
    (GATHER, 1, 2, 2),
    (PLANE_CORE, 1, 2, 1),
    (PLANE_X1, 0, 3),
    (PLANE_X1, 0, 2),
    (GATHER, 1, 1, 2),
    (PLANE_CORE, 1, 1, 1),
    (PLANE_X1, 0, 1),
    (PLANE_Y, 1, 3, 1),
    (PLANE_Y, 1, 2, 1),
    (GATHER, 1, 0, 4),
    (GRAD, 1, 0),
    (PLANE_CORE, 1, 2, 0),
    (GATHER, 1, 2, 3),
    (PLANE_Y, 1, 1, 1),
    (PLANE_X, 0, 0),
    (PLANE_Y, 1, 3, 0),
    (PLANE_END, 0, 1),
    (GATHER, 1, 1, 3),
    (PLANE_Y, 1, 2, 0),
    (PLANE_CORE, 1, 1, 0),
    (PLANE_CORE, 1, 0, 1),
    (PLANE_X1, 0, 0),
    (GATHER, 1, 2, 4),
    (GRAD, 1, 2),
    (PLANE_Y, 1, 1, 0),
    (PLANE_X, 1, 3),
    (GATHER, 1, 1, 4),
    (PLANE_CORE, 1, 0, 0),
    (PLANE_Y, 1, 0, 1),
    (PLANE_X, 1, 2),
    (PLANE_END, 0, 0),
    (PLANE_Y, 1, 0, 0),
    (PLANE_X, 1, 1),
    (PLANE_X1, 1, 3),
    (PLANE_END, 0, 3),
    (GRAD, 1, 1),
    (PLANE_X1, 1, 2),
    (PLANE_X, 1, 0),
    (PLANE_X1, 1, 1),
    (PLANE_END, 1, 3),
    (PLANE_X1, 1, 0),
    (PLANE_END, 1, 1),
    (PLANE_END, 0, 2),
    (PLANE_END, 1, 2),
    (PLANE_END, 1, 0),
)


def gelu_value(v):
    return 0.5 * v * (1.0 + lax.erf(v / math.sqrt(2.0)))


def gelu_slope(v):
    return 0.5 * (1.0 + lax.erf(v / math.sqrt(2.0))) + v * jnp.exp(
        -0.5 * v * v
    ) / math.sqrt(2.0 * math.pi)


def dot(left, right, ldim=1, rdim=0):
    return lax.dot_general(
        left, right, (((ldim,), (rdim,)), ((), ())), preferred_element_type=F32
    )


def kernel(
    normed,
    w_in,
    w_out,
    cot,
    o_block,
    o_gin,
    o_gwin,
    o_gwout,
    acts,
    wi,
    wo,
    hid,
    slope,
    zsend,
    zrecv,
    outp,
    crecv,
    ysend,
    yrecv,
    ysum,
    xsend,
    xrecv,
    gw,
    loc_sem,
    wl_sem,
    ag_send,
    ag_recv,
    w_send,
    w_recv,
    rs_send,
    rs_recv,
    za_send,
    za_recv,
    pl_send,
    pl_recv,
    gw_loc,
    gw_send,
    gw_recv,
):
    gx, gy, gz = lax.axis_index("gx"), lax.axis_index("gy"), lax.axis_index("gz")
    xl, z, xh, y, c = gx // 8, gx % 8, gy, gz // 2, gz % 2
    cy = c * 4 + y
    partner = ((1 - xl) * 8 + z, xh, gz)
    other = ((1 - xl) * 8 + z, 1 - xh, gz)
    opposite = (gx, 1 - xh, gz)
    zup = (xl * 8 + (z + 1) % 8, xh, gz)
    zdown = (xl * 8 + (z + 7) % 8, xh, gz)
    ynext = [(gx, xh, ((y + d) % 4) * 2 + c) for d in (1, 2, 3)]
    sibling = (gx, xh, y * 2 + 1 - c)

    def send(src, dst, ssem, rsem, dev):
        return pltpu.make_async_remote_copy(
            src_ref=src,
            dst_ref=dst,
            send_sem=ssem,
            recv_sem=rsem,
            device_id=dev,
            device_id_type=MESH,
        )

    def arrived(ref, ssem, rsem):
        send(ref, ref, ssem, rsem, sibling).wait_recv()

    def left_here(ref, ssem, rsem):
        send(ref, ref, ssem, rsem, sibling).wait_send()

    def span(start, size, unit=128):
        return pl.ds(pl.multiple_of(start, unit), size)

    def group(g):
        return pl.ds(g * GROUP, GROUP)

    ins = (normed, cot)
    my_cols = span(xl * 384, 384)
    its_cols = span((1 - xl) * 384, 384)

    def mine(t):
        b = (z + t + xh) % 2
        return b, span(((z + 4 - t + b * (2 * t + 1)) % 8) // 2 * 16, 16, 16)

    def local_piece(a, t):
        b, rows = mine(t)
        there = acts.at[a, 2 * t + b, cy, :, my_cols]
        return pltpu.make_async_copy(ins[a].at[rows, :], there, loc_sem.at[a, t])

    local_w = (
        pltpu.make_async_copy(
            w_in.at[:, span(xl * 768, 768)], wi.at[my_cols, :], wl_sem.at[0]
        ),
        pltpu.make_async_copy(
            w_out.at[span(xl * 768, 768), :], wo.at[:, my_cols], wl_sem.at[1]
        ),
    )
    for a in (0, 1):
        for t in range(4):
            local_piece(a, t).start()
        local_w[a].start()

    barrier = pltpu.get_barrier_semaphore()
    for dev in (partner, other, opposite, zup, zdown, *ynext, sibling):
        pl.semaphore_signal(barrier, inc=1, device_id=dev, device_id_type=MESH)
    pl.semaphore_wait(barrier, 9)

    def gather_x(a, t):
        b, _ = mine(t)
        there = acts.at[a, 2 * t + b, cy, :, my_cols]
        local_piece(a, t).wait()
        for m, dev in enumerate((partner, other, opposite)):
            sems = ag_send.at[a, t, m], ag_recv.at[a, t, m]
            send(there, there, *sems, dev).start()

    def gather_y(a, t):
        b, _ = mine(t)
        for m, (q, cols) in enumerate(
            ((b, its_cols), (1 - b, its_cols), (1 - b, my_cols))
        ):
            ref = acts.at[a, 2 * t + q, cy, :, cols]
            arrived(ref, ag_send.at[a, t, m], ag_recv.at[a, t, m])
        ref = acts.at[a, pl.ds(2 * t, 2), cy]
        for d in (0, 2, 1):
            sems = ag_send.at[a, t, 3 + d], ag_recv.at[a, t, 3 + d]
            send(ref, ref, *sems, ynext[d]).start()

    def gather_core(a, t):
        for d in range(3):
            ref = acts.at[a, pl.ds(2 * t, 2), c * 4 + (y + 3 - d) % 4]
            arrived(ref, ag_send.at[a, t, 3 + d], ag_recv.at[a, t, 3 + d])
        ref = acts.at[a, pl.ds(2 * t, 2), pl.ds(c * 4, 4)]
        send(ref, ref, ag_send.at[a, t, 6], ag_recv.at[a, t, 6], sibling).start()

    def gathered(a, t):
        ref = acts.at[a, pl.ds(2 * t, 2), pl.ds((1 - c) * 4, 4)]
        arrived(ref, ag_send.at[a, t, 6], ag_recv.at[a, t, 6])

    def swap_in(g):
        src = w_in.at[:, span((1 - xl) * 768 + g * GROUP, GROUP)]
        dst = wi.at[my_cols, group(g)]
        return send(src, dst, w_send.at[0, g], w_recv.at[0, g], partner)

    def swap_out(g):
        src = w_out.at[span((1 - xl) * 768 + g * GROUP, GROUP), :]
        dst = wo.at[group(g), my_cols]
        return send(src, dst, w_send.at[1, g], w_recv.at[1, g], partner)

    def w_arrived(p, g):
        if p == 0:
            ref = wi.at[its_cols, group(g)]
        else:
            ref = wo.at[group(g), its_cols]
        arrived(ref, w_send.at[p, g], w_recv.at[p, g])

    def term(p, g, slot):
        rows = acts[p, PLACE[slot]].reshape(CHUNK, DEPTH)
        if p == 0:
            return dot(rows, wi[:, group(g)])
        return dot(rows, wo[group(g), :], 1, 1)

    def ways(p, g):
        up, down = STEPS[(p + g) % 2]
        return ((up, 0, zup, 1), (down, up, zdown, -1))

    def reduce_step(p, g, s):
        for steps, first, dev, way in ways(p, g):
            if s >= steps:
                continue
            n = first + s
            total = term(p, g, way * (steps - s) % 8)
            if s > 0:
                got = zrecv.at[p, g, n - 1]
                sems = rs_send.at[p, g, n - 1], rs_recv.at[p, g, n - 1]
                arrived(got, *sems)
                left_here(got, *sems)
                total = total + got[...].astype(F32)
            zsend[p, g, n] = total.astype(BF)
            sems = rs_send.at[p, g, n], rs_recv.at[p, g, n]
            send(zsend.at[p, g, n], zrecv.at[p, g, n], *sems, dev).start()

    def share(p, g, slot):
        return hid.at[p, PLACE[slot % 8], :, group(g)]

    def reduce_end(p, g):
        total = term(p, g, 0)
        for steps, first, _, _ in ways(p, g):
            n = first + steps - 1
            got = zrecv.at[p, g, n]
            sems = rs_send.at[p, g, n], rs_recv.at[p, g, n]
            arrived(got, *sems)
            left_here(got, *sems)
            total = total + got[...].astype(F32)
        if p == 0:
            hid[0, PLACE[0], :, group(g)] = gelu_value(total).astype(BF)
            slope[:, group(g)] = gelu_slope(total)
        else:
            value = (total * slope[:, group(g)]).astype(BF)
            hid[1, PLACE[0], :, group(g)] = value
        gather_step(p, g, 0)

    def gather_step(p, g, s):
        for steps, first, dev, way in ways(p, g):
            if s > steps:
                continue
            n = first + s
            ref = share(p, g, -way * s)
            if s > 0:
                sems = za_send.at[p, g, n - 1], za_recv.at[p, g, n - 1]
                arrived(ref, *sems)
                left_here(ref, *sems)
            if s < steps:
                sems = za_send.at[p, g, n], za_recv.at[p, g, n]
                send(ref, share(p, g, -way * (s + 1)), *sems, dev).start()

    here = set()

    def need(p, *slots):
        for slot in slots:
            t = PLACE[slot % 8] // 2
            if (p, t) not in here:
                gathered(p, t)
                here.add((p, t))

    def reduce(p, g, s):
        if s == 0:
            if p not in here:
                local_w[p].wait()
                here.add(p)
            w_arrived(p, g)
        for steps, _, _, way in ways(p, g):
            if s < steps:
                need(p, way * (steps - s))
        if s < 4:
            reduce_step(p, g, s)
        else:
            need(p, 0)
            reduce_end(p, g)

    def plane_core(p, t, h):
        rows = hid[p, 2 * t + h]
        if p == 0:
            value = dot(rows, wo[...])
        else:
            value = dot(rows, wi[...], 1, 1)
        outp[p, t, h] = value.reshape(8, 16, DEPTH)
        src = outp.at[p, t, h, pl.ds((1 - c) * 4, 4)]
        sems = pl_send.at[p, t, h], pl_recv.at[p, t, h]
        send(src, crecv.at[p, t, h], *sems, sibling).start()

    def plane_y(p, t, h):
        sems = pl_send.at[p, t, h], pl_recv.at[p, t, h]
        arrived(crecv.at[p, t, h], *sems)
        for d in (0, 2, 1):
            at = (y + 1 + d) % 4
            value = outp[p, t, h, c * 4 + at] + crecv[p, t, h, at]
            ysend[p, t, d, h] = value.astype(BF)
            n = 2 + 3 * h + d
            sems = pl_send.at[p, t, n], pl_recv.at[p, t, n]
            send(ysend.at[p, t, d, h], yrecv.at[p, t, d, h], *sems, ynext[d]).start()

    def plane_x(p, t):
        total = outp[p, t, :, cy] + crecv[p, t, :, y]
        for d in range(3):
            for h in (0, 1):
                n = 2 + 3 * h + d
                sems = pl_send.at[p, t, n], pl_recv.at[p, t, n]
                arrived(yrecv.at[p, t, d, h], *sems)
            total = total + yrecv[p, t, d].astype(F32)
        ysum[p, t] = total
        b, _ = mine(t)
        for m, (q, cols, dev) in enumerate(
            (
                (1 - b, my_cols, opposite if direct(p, t) else other),
                (1 - b, its_cols, other),
                (b, its_cols, partner),
            )
        ):
            if m < 2 or direct(p, t):
                x_send(p, t, m, ysum.at[p, t, q, :, cols], dev)

    def direct(p, t):
        return p == 1 and t < DIRECT

    def x_send(p, t, m, src, dev):
        sems = pl_send.at[p, t, 8 + m], pl_recv.at[p, t, 8 + m]
        send(src, xrecv.at[p, t, m], *sems, dev).start()

    def x_arrived(p, t, m):
        sems = pl_send.at[p, t, 8 + m], pl_recv.at[p, t, 8 + m]
        arrived(xrecv.at[p, t, m], *sems)
        return xrecv[p, t, m]

    def plane_x1(p, t):
        b, _ = mine(t)
        xsend[p, t] = ysum[p, t, b, :, its_cols] + x_arrived(p, t, 0)
        x_send(p, t, 2, xsend.at[p, t], partner)

    def plane_end(p, t):
        b, rows = mine(t)
        total = ysum[p, t, b, :, my_cols]
        for m in (0, 1, 2) if direct(p, t) else (1, 2):
            total = total + x_arrived(p, t, m)
        (o_block, o_gin)[p][rows, :] = total.astype(BF)

    def grad_out(g):
        left = hid[0, :, :, group(g)].reshape(TOK, GROUP)
        value = dot(left, acts[1].reshape(TOK, DEPTH), 0, 0)
        gw[0, group(g), :] = value.astype(BF)
        there = o_gwout.at[span(xl * 768 + g * GROUP, GROUP), :]
        src = gw.at[0, group(g), its_cols]
        send(src, there, gw_send.at[0, g], gw_recv.at[0, g], partner).start()
        src = gw.at[0, group(g), my_cols]
        pltpu.make_async_copy(src, there, gw_loc.at[0, g]).start()

    def grad_in(g):
        right = hid[1, :, :, group(g)].reshape(TOK, GROUP)
        value = dot(acts[0].reshape(TOK, DEPTH), right, 0, 0)
        gw[1, :, group(g)] = value.astype(BF)
        there = o_gwin.at[:, span(xl * 768 + g * GROUP, GROUP)]
        src = gw.at[1, its_cols, group(g)]
        send(src, there, gw_send.at[1, g], gw_recv.at[1, g], partner).start()
        src = gw.at[1, my_cols, group(g)]
        pltpu.make_async_copy(src, there, gw_loc.at[1, g]).start()

    def grad(p, g):
        need(1 - p, *range(8))
        (grad_out, grad_in)[p](g)

    def grads_end():
        for g in range(GROUPS):
            ref = gw.at[0, group(g), its_cols]
            here = o_gwout.at[span((1 - xl) * 768 + g * GROUP, GROUP), :]
            pltpu.make_async_copy(ref, here, gw_loc.at[0, g]).wait()
            left_here(ref, gw_send.at[0, g], gw_recv.at[0, g])
            arrived(here, gw_send.at[0, g], gw_recv.at[0, g])
            ref = gw.at[1, its_cols, group(g)]
            here = o_gwin.at[:, span((1 - xl) * 768 + g * GROUP, GROUP)]
            pltpu.make_async_copy(ref, here, gw_loc.at[1, g]).wait()
            left_here(ref, gw_send.at[1, g], gw_recv.at[1, g])
            arrived(here, gw_send.at[1, g], gw_recv.at[1, g])

    def inputs_left(a):
        for t in range(4):
            for m in range(3):
                ref = acts.at[a, 0, 0, :, pl.ds(0, 384)]
                left_here(ref, ag_send.at[a, t, m], ag_recv.at[a, t, m])
                ref = acts.at[a, pl.ds(0, 2), 0]
                left_here(ref, ag_send.at[a, t, 3 + m], ag_recv.at[a, t, 3 + m])
            ref = acts.at[a, pl.ds(0, 2), pl.ds(0, 4)]
            left_here(ref, ag_send.at[a, t, 6], ag_recv.at[a, t, 6])

    def weights_left():
        for g in range(GROUPS):
            left_here(wi.at[my_cols, group(g)], w_send.at[0, g], w_recv.at[0, g])
            left_here(wo.at[group(g), my_cols], w_send.at[1, g], w_recv.at[1, g])

    def plane_left(p):
        for t in range(4):
            for h in (0, 1):
                sems = pl_send.at[p, t, h], pl_recv.at[p, t, h]
                left_here(crecv.at[p, t, h], *sems)
                for d in range(3):
                    n = 2 + 3 * h + d
                    sems = pl_send.at[p, t, n], pl_recv.at[p, t, n]
                    left_here(ysend.at[p, t, d, h], *sems)
            for m in range(3):
                sems = pl_send.at[p, t, 8 + m], pl_recv.at[p, t, 8 + m]
                left_here(xrecv.at[p, t, m], *sems)

    for t in range(4):
        gather_x(0, t)
    swap_in(0).start()
    for t in range(4):
        gather_x(1, t)
    for g in range(1, GROUPS):
        swap_in(g).start()
    for g in range(GROUPS):
        swap_out(g).start()
    table = {
        GATHER_Y: gather_y,
        GATHER_CORE: gather_core,
        REDUCE: reduce,
        GATHER: gather_step,
        GRAD: grad,
        PLANE_CORE: plane_core,
        PLANE_Y: plane_y,
        PLANE_X: plane_x,
        PLANE_X1: plane_x1,
        PLANE_END: plane_end,
    }
    for what, *where in SCHEDULE:
        table[what](*where)
    weights_left()
    for a in (0, 1):
        inputs_left(a)
        plane_left(a)
    grads_end()


def settle(*refs):
    ins, outs, held, sems = refs[:4], refs[4:8], refs[8:12], refs[12]
    loads = [pltpu.make_async_copy(ins[i], held[i], sems.at[0, i]) for i in range(4)]
    stores = [pltpu.make_async_copy(held[i], outs[i], sems.at[1, i]) for i in range(4)]
    for i in (2, 3, 0, 1):
        loads[i].start()
    for i in (2, 3, 0, 1):
        loads[i].wait()
        stores[i].start()
    for store in stores:
        store.wait()


def shards(normed, w_in, w_out, cotangent):
    hbm = pl.BlockSpec(memory_space=pltpu.HBM)
    vmem = pl.BlockSpec(memory_space=pltpu.VMEM)
    dma = pltpu.SemaphoreType.DMA
    shapes = (
        jax.ShapeDtypeStruct((64, 384), BF),
        jax.ShapeDtypeStruct((64, 384), BF),
        jax.ShapeDtypeStruct((384, 1536), BF),
        jax.ShapeDtypeStruct((1536, 384), BF),
    )
    results = pl.pallas_call(
        kernel,
        out_shape=shapes,
        in_specs=[hbm] * 4,
        out_specs=(vmem, vmem, hbm, hbm),
        scratch_shapes=[
            pltpu.VMEM((2, 8, 8, 16, DEPTH), BF),
            pltpu.VMEM((DEPTH, UNITS), BF),
            pltpu.VMEM((UNITS, DEPTH), BF),
            pltpu.VMEM((2, 8, CHUNK, UNITS), BF),
            pltpu.VMEM((CHUNK, UNITS), F32),
            pltpu.VMEM((2, GROUPS, 7, CHUNK, GROUP), BF),
            pltpu.VMEM((2, GROUPS, 7, CHUNK, GROUP), BF),
            pltpu.VMEM((2, 4, 2, 8, 16, DEPTH), F32),
            pltpu.VMEM((2, 4, 2, 4, 16, DEPTH), F32),
            pltpu.VMEM((2, 4, 3, 2, 16, DEPTH), BF),
            pltpu.VMEM((2, 4, 3, 2, 16, DEPTH), BF),
            pltpu.VMEM((2, 4, 2, 16, DEPTH), F32),
            pltpu.VMEM((2, 4, 16, 384), F32),
            pltpu.VMEM((2, 4, 3, 16, 384), F32),
            pltpu.VMEM((2, DEPTH, UNITS), BF),
            dma((2, 4)),
            dma((2,)),
            dma((2, 4, 7)),
            dma((2, 4, 7)),
            dma((2, GROUPS)),
            dma((2, GROUPS)),
            dma((2, GROUPS, 7)),
            dma((2, GROUPS, 7)),
            dma((2, GROUPS, 7)),
            dma((2, GROUPS, 7)),
            dma((2, 4, 11)),
            dma((2, 4, 11)),
            dma((2, GROUPS)),
            dma((2, GROUPS)),
            dma((2, GROUPS)),
        ],
        compiler_params=pltpu.CompilerParams(
            collective_id=0,
            has_side_effects=True,
            vmem_limit_bytes=58 * 1024 * 1024,
        ),
        cost_estimate=pl.CostEstimate(
            flops=7_247_757_312, bytes_accessed=5_000_000, transcendentals=400_000
        ),
    )(normed, w_in, w_out, cotangent)
    return pl.pallas_call(
        settle,
        out_shape=shapes,
        in_specs=[hbm] * 4,
        out_specs=(hbm,) * 4,
        scratch_shapes=[
            *(pltpu.VMEM(shape.shape, BF) for shape in shapes),
            dma((2, 4)),
        ],
        cost_estimate=pl.CostEstimate(
            flops=0, bytes_accessed=4_900_000, transcendentals=0
        ),
    )(*results)


def solution(mesh):
    return jax.shard_map(
        shards,
        mesh=mesh,
        in_specs=(
            P(("gy", "gz"), "gx"),
            P("gx", ("gz", "gy")),
            P(("gz", "gy"), "gx"),
            P(("gy", "gz"), "gx"),
        ),
        out_specs=(
            P(("gy", "gz"), "gx"),
            P(("gy", "gz"), "gx"),
            P("gx", ("gz", "gy")),
            P(("gz", "gy"), "gx"),
        ),
        check_vma=False,
    )
```

```python
import math

import jax
import jax.numpy as jnp
from jax import lax
from jax.experimental import pallas as pl
from jax.experimental.pallas import tpu as pltpu
from jax.sharding import PartitionSpec as P

BF = jnp.bfloat16
F32 = jnp.float32
MESH = pl.DeviceIdType.MESH

TOK = 1024
CHUNK = 128
DEPTH = 768
UNITS = 768
GROUP = 256
GROUPS = 3
STEPS = ((4, 3), (3, 4))
PLACE = (7, 6, 4, 2, 0, 1, 3, 5)
DIRECT = 0


GATHER_Y, GATHER_CORE, REDUCE, GATHER, GRAD = range(5)
PLANE_CORE, PLANE_Y, PLANE_X, PLANE_X1, PLANE_END = range(5, 10)
SCHEDULE = (
    (GATHER_Y, 0, 0),
    (GATHER_Y, 0, 1),
    (GATHER_Y, 0, 2),
    (GATHER_Y, 0, 3),
    (GATHER_CORE, 0, 0),
    (REDUCE, 0, 0, 0),
    (GATHER_Y, 1, 1),
    (GATHER_CORE, 0, 1),
    (REDUCE, 0, 0, 1),
    (GATHER_Y, 1, 0),
    (GATHER_CORE, 0, 2),
    (REDUCE, 0, 1, 0),
    (GATHER_Y, 1, 3),
    (REDUCE, 0, 0, 2),
    (GATHER_CORE, 0, 3),
    (GATHER_CORE, 1, 1),
    (REDUCE, 0, 1, 1),
    (REDUCE, 0, 2, 0),
    (REDUCE, 0, 0, 3),
    (REDUCE, 0, 1, 2),
    (GATHER_Y, 1, 2),
    (REDUCE, 0, 2, 1),
    (GATHER_CORE, 1, 0),
    (REDUCE, 0, 0, 4),
    (GATHER_CORE, 1, 3),
    (REDUCE, 1, 0, 0),
    (REDUCE, 0, 2, 2),
    (GATHER, 0, 0, 1),
    (GATHER_CORE, 1, 2),
    (REDUCE, 0, 1, 3),
    (REDUCE, 1, 1, 0),
    (REDUCE, 0, 2, 3),
    (REDUCE, 1, 2, 0),
    (REDUCE, 0, 1, 4),
    (REDUCE, 0, 2, 4),
    (REDUCE, 1, 0, 1),
    (REDUCE, 1, 2, 1),
    (GATHER, 0, 0, 2),
    (GATHER, 0, 2, 1),
    (GATHER, 0, 1, 1),
    (REDUCE, 1, 2, 2),
    (GATHER, 0, 0, 3),
    (REDUCE, 1, 0, 2),
    (REDUCE, 1, 1, 1),
    (PLANE_CORE, 0, 3, 0),
    (GATHER, 0, 2, 2),
    (REDUCE, 1, 0, 3),
    (GATHER, 0, 1, 2),
    (GATHER, 0, 0, 4),
    (PLANE_CORE, 0, 2, 1),
    (PLANE_Y, 0, 3, 0),
    (PLANE_CORE, 0, 1, 1),
    (PLANE_CORE, 0, 3, 1),
    (GRAD, 0, 0),
    (REDUCE, 1, 1, 2),
    (REDUCE, 1, 0, 4),
    (REDUCE, 1, 2, 3),
    (PLANE_CORE, 0, 2, 0),
    (PLANE_Y, 0, 3, 1),
    (GATHER, 0, 2, 3),
    (PLANE_Y, 0, 2, 0),
    (GATHER, 0, 1, 3),
    (REDUCE, 1, 1, 3),
    (PLANE_Y, 0, 1, 1),
    (PLANE_CORE, 0, 1, 0),
    (GATHER, 1, 0, 1),
    (PLANE_Y, 0, 2, 1),
    (REDUCE, 1, 2, 4),
    (GATHER, 0, 2, 4),
    (GRAD, 0, 2),
    (PLANE_Y, 0, 1, 0),
    (GATHER, 0, 1, 4),
    (REDUCE, 1, 1, 4),
    (PLANE_CORE, 0, 0, 1),
    (GRAD, 0, 1),
    (GATHER, 1, 0, 2),
    (PLANE_X, 0, 3),
    (PLANE_CORE, 0, 0, 0),
    (GATHER, 1, 2, 1),
    (PLANE_Y, 0, 0, 1),
    (PLANE_Y, 0, 0, 0),
    (GATHER, 1, 1, 1),
    (PLANE_CORE, 1, 3, 1),
    (PLANE_X, 0, 2),
    (PLANE_X, 0, 1),
    (PLANE_CORE, 1, 3, 0),
    (GATHER, 1, 0, 3),
    (GATHER, 1, 2, 2),
    (PLANE_CORE, 1, 2, 1),
    (PLANE_X1, 0, 3),
    (PLANE_X1, 0, 2),
    (GATHER, 1, 1, 2),
    (PLANE_CORE, 1, 1, 1),
    (PLANE_X1, 0, 1),
    (PLANE_Y, 1, 3, 1),
    (PLANE_Y, 1, 2, 1),
    (GATHER, 1, 0, 4),
    (GRAD, 1, 0),
    (PLANE_CORE, 1, 2, 0),
    (GATHER, 1, 2, 3),
    (PLANE_Y, 1, 1, 1),
    (PLANE_X, 0, 0),
    (PLANE_Y, 1, 3, 0),
    (PLANE_END, 0, 1),
    (GATHER, 1, 1, 3),
    (PLANE_Y, 1, 2, 0),
    (PLANE_CORE, 1, 1, 0),
    (PLANE_CORE, 1, 0, 1),
    (PLANE_X1, 0, 0),
    (GATHER, 1, 2, 4),
    (GRAD, 1, 2),
    (PLANE_Y, 1, 1, 0),
    (PLANE_X, 1, 3),
    (GATHER, 1, 1, 4),
    (PLANE_CORE, 1, 0, 0),
    (PLANE_Y, 1, 0, 1),
    (PLANE_X, 1, 2),
    (PLANE_END, 0, 0),
    (PLANE_Y, 1, 0, 0),
    (PLANE_X, 1, 1),
    (PLANE_X1, 1, 3),
    (PLANE_END, 0, 3),
    (GRAD, 1, 1),
    (PLANE_X1, 1, 2),
    (PLANE_X, 1, 0),
    (PLANE_X1, 1, 1),
    (PLANE_END, 1, 3),
    (PLANE_X1, 1, 0),
    (PLANE_END, 1, 1),
    (PLANE_END, 0, 2),
    (PLANE_END, 1, 2),
    (PLANE_END, 1, 0),
)


def gelu_value(v):
    return 0.5 * v * (1.0 + lax.erf(v / math.sqrt(2.0)))


def gelu_slope(v):
    return 0.5 * (1.0 + lax.erf(v / math.sqrt(2.0))) + v * jnp.exp(
        -0.5 * v * v
    ) / math.sqrt(2.0 * math.pi)


def dot(left, right, ldim=1, rdim=0):
    return lax.dot_general(
        left, right, (((ldim,), (rdim,)), ((), ())), preferred_element_type=F32
    )


def kernel(
    normed,
    w_in,
    w_out,
    cot,
    o_block,
    o_gin,
    o_gwin,
    o_gwout,
    acts,
    wi,
    wo,
    hid,
    slope,
    zsend,
    zrecv,
    outp,
    crecv,
    ysend,
    yrecv,
    ysum,
    xsend,
    xrecv,
    gw,
    loc_sem,
    wl_sem,
    ag_send,
    ag_recv,
    w_send,
    w_recv,
    rs_send,
    rs_recv,
    za_send,
    za_recv,
    pl_send,
    pl_recv,
    gw_loc,
    gw_send,
    gw_recv,
):
    gx, gy, gz = lax.axis_index("gx"), lax.axis_index("gy"), lax.axis_index("gz")
    xl, z, xh, y, c = gx // 8, gx % 8, gy, gz // 2, gz % 2
    cy = c * 4 + y
    partner = ((1 - xl) * 8 + z, xh, gz)
    other = ((1 - xl) * 8 + z, 1 - xh, gz)
    opposite = (gx, 1 - xh, gz)
    zup = (xl * 8 + (z + 1) % 8, xh, gz)
    zdown = (xl * 8 + (z + 7) % 8, xh, gz)
    ynext = [(gx, xh, ((y + d) % 4) * 2 + c) for d in (1, 2, 3)]
    sibling = (gx, xh, y * 2 + 1 - c)

    def send(src, dst, ssem, rsem, dev):
        return pltpu.make_async_remote_copy(
            src_ref=src,
            dst_ref=dst,
            send_sem=ssem,
            recv_sem=rsem,
            device_id=dev,
            device_id_type=MESH,
        )

    def arrived(ref, ssem, rsem):
        send(ref, ref, ssem, rsem, sibling).wait_recv()

    def left_here(ref, ssem, rsem):
        send(ref, ref, ssem, rsem, sibling).wait_send()

    def span(start, size, unit=128):
        return pl.ds(pl.multiple_of(start, unit), size)

    def group(g):
        return pl.ds(g * GROUP, GROUP)

    ins = (normed, cot)
    my_cols = span(xl * 384, 384)
    its_cols = span((1 - xl) * 384, 384)

    def mine(t):
        b = (z + t + xh) % 2
        return b, span(((z + 4 - t + b * (2 * t + 1)) % 8) // 2 * 16, 16, 16)

    def local_piece(a, t):
        b, rows = mine(t)
        there = acts.at[a, 2 * t + b, cy, :, my_cols]
        return pltpu.make_async_copy(ins[a].at[rows, :], there, loc_sem.at[a, t])

    local_w = (
        pltpu.make_async_copy(
            w_in.at[:, span(xl * 768, 768)], wi.at[my_cols, :], wl_sem.at[0]
        ),
        pltpu.make_async_copy(
            w_out.at[span(xl * 768, 768), :], wo.at[:, my_cols], wl_sem.at[1]
        ),
    )
    for a in (0, 1):
        for t in range(4):
            local_piece(a, t).start()
        local_w[a].start()

    barrier = pltpu.get_barrier_semaphore()
    for dev in (partner, other, opposite, zup, zdown, *ynext, sibling):
        pl.semaphore_signal(barrier, inc=1, device_id=dev, device_id_type=MESH)
    pl.semaphore_wait(barrier, 9)

    def gather_x(a, t):
        b, _ = mine(t)
        there = acts.at[a, 2 * t + b, cy, :, my_cols]
        local_piece(a, t).wait()
        for m, dev in enumerate((partner, other, opposite)):
            sems = ag_send.at[a, t, m], ag_recv.at[a, t, m]
            send(there, there, *sems, dev).start()

    def gather_y(a, t):
        b, _ = mine(t)
        for m, (q, cols) in enumerate(
            ((b, its_cols), (1 - b, its_cols), (1 - b, my_cols))
        ):
            ref = acts.at[a, 2 * t + q, cy, :, cols]
            arrived(ref, ag_send.at[a, t, m], ag_recv.at[a, t, m])
        ref = acts.at[a, pl.ds(2 * t, 2), cy]
        for d in (0, 2, 1):
            sems = ag_send.at[a, t, 3 + d], ag_recv.at[a, t, 3 + d]
            send(ref, ref, *sems, ynext[d]).start()

    def gather_core(a, t):
        for d in range(3):
            ref = acts.at[a, pl.ds(2 * t, 2), c * 4 + (y + 3 - d) % 4]
            arrived(ref, ag_send.at[a, t, 3 + d], ag_recv.at[a, t, 3 + d])
        ref = acts.at[a, pl.ds(2 * t, 2), pl.ds(c * 4, 4)]
        send(ref, ref, ag_send.at[a, t, 6], ag_recv.at[a, t, 6], sibling).start()

    def gathered(a, t):
        ref = acts.at[a, pl.ds(2 * t, 2), pl.ds((1 - c) * 4, 4)]
        arrived(ref, ag_send.at[a, t, 6], ag_recv.at[a, t, 6])

    def swap_in(g):
        src = w_in.at[:, span((1 - xl) * 768 + g * GROUP, GROUP)]
        dst = wi.at[my_cols, group(g)]
        return send(src, dst, w_send.at[0, g], w_recv.at[0, g], partner)

    def swap_out(g):
        src = w_out.at[span((1 - xl) * 768 + g * GROUP, GROUP), :]
        dst = wo.at[group(g), my_cols]
        return send(src, dst, w_send.at[1, g], w_recv.at[1, g], partner)

    def w_arrived(p, g):
        if p == 0:
            ref = wi.at[its_cols, group(g)]
        else:
            ref = wo.at[group(g), its_cols]
        arrived(ref, w_send.at[p, g], w_recv.at[p, g])

    def term(p, g, slot):
        rows = acts[p, PLACE[slot]].reshape(CHUNK, DEPTH)
        if p == 0:
            return dot(rows, wi[:, group(g)])
        return dot(rows, wo[group(g), :], 1, 1)

    def ways(p, g):
        up, down = STEPS[(p + g) % 2]
        return ((up, 0, zup, 1), (down, up, zdown, -1))

    def reduce_step(p, g, s):
        for steps, first, dev, way in ways(p, g):
            if s >= steps:
                continue
            n = first + s
            total = term(p, g, way * (steps - s) % 8)
            if s > 0:
                got = zrecv.at[p, g, n - 1]
                sems = rs_send.at[p, g, n - 1], rs_recv.at[p, g, n - 1]
                arrived(got, *sems)
                left_here(got, *sems)
                total = total + got[...].astype(F32)
            zsend[p, g, n] = total.astype(BF)
            sems = rs_send.at[p, g, n], rs_recv.at[p, g, n]
            send(zsend.at[p, g, n], zrecv.at[p, g, n], *sems, dev).start()

    def share(p, g, slot):
        return hid.at[p, PLACE[slot % 8], :, group(g)]

    def reduce_end(p, g):
        total = term(p, g, 0)
        for steps, first, _, _ in ways(p, g):
            n = first + steps - 1
            got = zrecv.at[p, g, n]
            sems = rs_send.at[p, g, n], rs_recv.at[p, g, n]
            arrived(got, *sems)
            left_here(got, *sems)
            total = total + got[...].astype(F32)
        if p == 0:
            hid[0, PLACE[0], :, group(g)] = gelu_value(total).astype(BF)
            slope[:, group(g)] = gelu_slope(total)
        else:
            value = (total * slope[:, group(g)]).astype(BF)
            hid[1, PLACE[0], :, group(g)] = value
        gather_step(p, g, 0)

    def gather_step(p, g, s):
        for steps, first, dev, way in ways(p, g):
            if s > steps:
                continue
            n = first + s
            ref = share(p, g, -way * s)
            if s > 0:
                sems = za_send.at[p, g, n - 1], za_recv.at[p, g, n - 1]
                arrived(ref, *sems)
                left_here(ref, *sems)
            if s < steps:
                sems = za_send.at[p, g, n], za_recv.at[p, g, n]
                send(ref, share(p, g, -way * (s + 1)), *sems, dev).start()

    here = set()

    def need(p, *slots):
        for slot in slots:
            t = PLACE[slot % 8] // 2
            if (p, t) not in here:
                gathered(p, t)
                here.add((p, t))

    def reduce(p, g, s):
        if s == 0:
            if p not in here:
                local_w[p].wait()
                here.add(p)
            w_arrived(p, g)
        for steps, _, _, way in ways(p, g):
            if s < steps:
                need(p, way * (steps - s))
        if s < 4:
            reduce_step(p, g, s)
        else:
            need(p, 0)
            reduce_end(p, g)

    def plane_core(p, t, h):
        rows = hid[p, 2 * t + h]
        if p == 0:
            value = dot(rows, wo[...])
        else:
            value = dot(rows, wi[...], 1, 1)
        outp[p, t, h] = value.reshape(8, 16, DEPTH)
        src = outp.at[p, t, h, pl.ds((1 - c) * 4, 4)]
        sems = pl_send.at[p, t, h], pl_recv.at[p, t, h]
        send(src, crecv.at[p, t, h], *sems, sibling).start()

    def plane_y(p, t, h):
        sems = pl_send.at[p, t, h], pl_recv.at[p, t, h]
        arrived(crecv.at[p, t, h], *sems)
        for d in (0, 2, 1):
            at = (y + 1 + d) % 4
            value = outp[p, t, h, c * 4 + at] + crecv[p, t, h, at]
            ysend[p, t, d, h] = value.astype(BF)
            n = 2 + 3 * h + d
            sems = pl_send.at[p, t, n], pl_recv.at[p, t, n]
            send(ysend.at[p, t, d, h], yrecv.at[p, t, d, h], *sems, ynext[d]).start()

    def plane_x(p, t):
        total = outp[p, t, :, cy] + crecv[p, t, :, y]
        for d in range(3):
            for h in (0, 1):
                n = 2 + 3 * h + d
                sems = pl_send.at[p, t, n], pl_recv.at[p, t, n]
                arrived(yrecv.at[p, t, d, h], *sems)
            total = total + yrecv[p, t, d].astype(F32)
        ysum[p, t] = total
        b, _ = mine(t)
        for m, (q, cols, dev) in enumerate(
            (
                (1 - b, my_cols, opposite if direct(p, t) else other),
                (1 - b, its_cols, other),
                (b, its_cols, partner),
            )
        ):
            if m < 2 or direct(p, t):
                x_send(p, t, m, ysum.at[p, t, q, :, cols], dev)

    def direct(p, t):
        return p == 1 and t < DIRECT

    def x_send(p, t, m, src, dev):
        sems = pl_send.at[p, t, 8 + m], pl_recv.at[p, t, 8 + m]
        send(src, xrecv.at[p, t, m], *sems, dev).start()

    def x_arrived(p, t, m):
        sems = pl_send.at[p, t, 8 + m], pl_recv.at[p, t, 8 + m]
        arrived(xrecv.at[p, t, m], *sems)
        return xrecv[p, t, m]

    def plane_x1(p, t):
        b, _ = mine(t)
        xsend[p, t] = ysum[p, t, b, :, its_cols] + x_arrived(p, t, 0)
        x_send(p, t, 2, xsend.at[p, t], partner)

    def plane_end(p, t):
        b, rows = mine(t)
        total = ysum[p, t, b, :, my_cols]
        for m in (0, 1, 2) if direct(p, t) else (1, 2):
            total = total + x_arrived(p, t, m)
        (o_block, o_gin)[p][rows, :] = total.astype(BF)

    def grad_out(g):
        left = hid[0, :, :, group(g)].reshape(TOK, GROUP)
        value = dot(left, acts[1].reshape(TOK, DEPTH), 0, 0)
        gw[0, group(g), :] = value.astype(BF)
        there = o_gwout.at[span(xl * 768 + g * GROUP, GROUP), :]
        src = gw.at[0, group(g), its_cols]
        send(src, there, gw_send.at[0, g], gw_recv.at[0, g], partner).start()
        src = gw.at[0, group(g), my_cols]
        pltpu.make_async_copy(src, there, gw_loc.at[0, g]).start()

    def grad_in(g):
        right = hid[1, :, :, group(g)].reshape(TOK, GROUP)
        value = dot(acts[0].reshape(TOK, DEPTH), right, 0, 0)
        gw[1, :, group(g)] = value.astype(BF)
        there = o_gwin.at[:, span(xl * 768 + g * GROUP, GROUP)]
        src = gw.at[1, its_cols, group(g)]
        send(src, there, gw_send.at[1, g], gw_recv.at[1, g], partner).start()
        src = gw.at[1, my_cols, group(g)]
        pltpu.make_async_copy(src, there, gw_loc.at[1, g]).start()

    def grad(p, g):
        need(1 - p, *range(8))
        (grad_out, grad_in)[p](g)

    def grads_end():
        for g in range(GROUPS):
            ref = gw.at[0, group(g), its_cols]
            here = o_gwout.at[span((1 - xl) * 768 + g * GROUP, GROUP), :]
            pltpu.make_async_copy(ref, here, gw_loc.at[0, g]).wait()
            left_here(ref, gw_send.at[0, g], gw_recv.at[0, g])
            arrived(here, gw_send.at[0, g], gw_recv.at[0, g])
            ref = gw.at[1, its_cols, group(g)]
            here = o_gwin.at[:, span((1 - xl) * 768 + g * GROUP, GROUP)]
            pltpu.make_async_copy(ref, here, gw_loc.at[1, g]).wait()
            left_here(ref, gw_send.at[1, g], gw_recv.at[1, g])
            arrived(here, gw_send.at[1, g], gw_recv.at[1, g])

    def inputs_left(a):
        for t in range(4):
            for m in range(3):
                ref = acts.at[a, 0, 0, :, pl.ds(0, 384)]
                left_here(ref, ag_send.at[a, t, m], ag_recv.at[a, t, m])
                ref = acts.at[a, pl.ds(0, 2), 0]
                left_here(ref, ag_send.at[a, t, 3 + m], ag_recv.at[a, t, 3 + m])
            ref = acts.at[a, pl.ds(0, 2), pl.ds(0, 4)]
            left_here(ref, ag_send.at[a, t, 6], ag_recv.at[a, t, 6])

    def weights_left():
        for g in range(GROUPS):
            left_here(wi.at[my_cols, group(g)], w_send.at[0, g], w_recv.at[0, g])
            left_here(wo.at[group(g), my_cols], w_send.at[1, g], w_recv.at[1, g])

    def plane_left(p):
        for t in range(4):
            for h in (0, 1):
                sems = pl_send.at[p, t, h], pl_recv.at[p, t, h]
                left_here(crecv.at[p, t, h], *sems)
                for d in range(3):
                    n = 2 + 3 * h + d
                    sems = pl_send.at[p, t, n], pl_recv.at[p, t, n]
                    left_here(ysend.at[p, t, d, h], *sems)
            for m in range(3):
                sems = pl_send.at[p, t, 8 + m], pl_recv.at[p, t, 8 + m]
                left_here(xrecv.at[p, t, m], *sems)

    for t in range(4):
        gather_x(0, t)
    swap_in(0).start()
    for t in range(4):
        gather_x(1, t)
    for g in range(1, GROUPS):
        swap_in(g).start()
    for g in range(GROUPS):
        swap_out(g).start()
    table = {
        GATHER_Y: gather_y,
        GATHER_CORE: gather_core,
        REDUCE: reduce,
        GATHER: gather_step,
        GRAD: grad,
        PLANE_CORE: plane_core,
        PLANE_Y: plane_y,
        PLANE_X: plane_x,
        PLANE_X1: plane_x1,
        PLANE_END: plane_end,
    }
    for what, *where in SCHEDULE:
        table[what](*where)
    weights_left()
    for a in (0, 1):
        inputs_left(a)
        plane_left(a)
    grads_end()


def settle(*refs):
    ins, outs, held, sems = refs[:4], refs[4:8], refs[8:12], refs[12]
    parts = [(i, pl.ds(n * rows, rows)) for n in range(4) for i, rows in ((2, 96), (3, 384))]
    parts += [(0, pl.ds(0, 64)), (1, pl.ds(0, 64))]
    loads = [
        pltpu.make_async_copy(ins[i].at[at, :], held[i].at[at, :], sems.at[0, n])
        for n, (i, at) in enumerate(parts)
    ]
    stores = [
        pltpu.make_async_copy(held[i].at[at, :], outs[i].at[at, :], sems.at[1, n])
        for n, (i, at) in enumerate(parts)
    ]
    for load in loads:
        load.start()
    for load, store in zip(loads, stores):
        load.wait()
        store.start()
    for store in stores:
        store.wait()


def shards(normed, w_in, w_out, cotangent):
    hbm = pl.BlockSpec(memory_space=pltpu.HBM)
    vmem = pl.BlockSpec(memory_space=pltpu.VMEM)
    dma = pltpu.SemaphoreType.DMA
    shapes = (
        jax.ShapeDtypeStruct((64, 384), BF),
        jax.ShapeDtypeStruct((64, 384), BF),
        jax.ShapeDtypeStruct((384, 1536), BF),
        jax.ShapeDtypeStruct((1536, 384), BF),
    )
    results = pl.pallas_call(
        kernel,
        out_shape=shapes,
        in_specs=[hbm] * 4,
        out_specs=(vmem, vmem, hbm, hbm),
        scratch_shapes=[
            pltpu.VMEM((2, 8, 8, 16, DEPTH), BF),
            pltpu.VMEM((DEPTH, UNITS), BF),
            pltpu.VMEM((UNITS, DEPTH), BF),
            pltpu.VMEM((2, 8, CHUNK, UNITS), BF),
            pltpu.VMEM((CHUNK, UNITS), F32),
            pltpu.VMEM((2, GROUPS, 7, CHUNK, GROUP), BF),
            pltpu.VMEM((2, GROUPS, 7, CHUNK, GROUP), BF),
            pltpu.VMEM((2, 4, 2, 8, 16, DEPTH), F32),
            pltpu.VMEM((2, 4, 2, 4, 16, DEPTH), F32),
            pltpu.VMEM((2, 4, 3, 2, 16, DEPTH), BF),
            pltpu.VMEM((2, 4, 3, 2, 16, DEPTH), BF),
            pltpu.VMEM((2, 4, 2, 16, DEPTH), F32),
            pltpu.VMEM((2, 4, 16, 384), F32),
            pltpu.VMEM((2, 4, 3, 16, 384), F32),
            pltpu.VMEM((2, DEPTH, UNITS), BF),
            dma((2, 4)),
            dma((2,)),
            dma((2, 4, 7)),
            dma((2, 4, 7)),
            dma((2, GROUPS)),
            dma((2, GROUPS)),
            dma((2, GROUPS, 7)),
            dma((2, GROUPS, 7)),
            dma((2, GROUPS, 7)),
            dma((2, GROUPS, 7)),
            dma((2, 4, 11)),
            dma((2, 4, 11)),
            dma((2, GROUPS)),
            dma((2, GROUPS)),
            dma((2, GROUPS)),
        ],
        compiler_params=pltpu.CompilerParams(
            collective_id=0,
            has_side_effects=True,
            vmem_limit_bytes=58 * 1024 * 1024,
        ),
        cost_estimate=pl.CostEstimate(
            flops=7_247_757_312, bytes_accessed=5_000_000, transcendentals=400_000
        ),
    )(normed, w_in, w_out, cotangent)
    return pl.pallas_call(
        settle,
        out_shape=shapes,
        in_specs=[hbm] * 4,
        out_specs=(hbm,) * 4,
        scratch_shapes=[
            *(pltpu.VMEM(shape.shape, BF) for shape in shapes),
            dma((2, 10)),
        ],
        cost_estimate=pl.CostEstimate(
            flops=0, bytes_accessed=4_900_000, transcendentals=0
        ),
    )(*results)


def solution(mesh):
    return jax.shard_map(
        shards,
        mesh=mesh,
        in_specs=(
            P(("gy", "gz"), "gx"),
            P("gx", ("gz", "gy")),
            P(("gz", "gy"), "gx"),
            P(("gy", "gz"), "gx"),
        ),
        out_specs=(
            P(("gy", "gz"), "gx"),
            P(("gy", "gz"), "gx"),
            P("gx", ("gz", "gy")),
            P(("gz", "gy"), "gx"),
        ),
        check_vma=False,
    )
```
